32 devices in a mesh: gx: 4 (over x, core), gy: 2 (over y), gz: 4 (over z).
Axes of the slice: x: 2, y: 2, z: 4, core: 2. Of those that a mesh axis runs over, the one named last changes fastest.
Arguments:
- density: float32 [32, 256, 512], P('gz', 'gx', 'gy'), may hold values from 0.2 to 2
- bins: int32 [32, 256, 512], P('gz', 'gx', 'gy'), may hold values from 0 to 255
- colour_table: bfloat16 [3, 256], replicated, may hold values from 0.049804688 to 1
- opacity_table: bfloat16 [256], replicated, may hold values from 0.19921875 to 2.5
- order: int32 [4, 2, 4], P('gx', 'gy'), may hold values from 0 to 3, each once within a row
Outputs:
- image: float32 [4, 256, 512], P(None, ('gx', 'gz'), 'gy')
The draws below stay inside these ranges and needn't reach their ends.
Inputs may be any that keep to these rules, and one draw needn't show every extreme that they name: For each column block and row block, order holds each brick rank 0 to 3 once.
All inputs are finite; a program needn't handle non-finite values.
Results may differ from the reference program's by a relative error of at most 0.0003.
Values sent between devices are 32-bit elements; how exact they have to be, the bound alone decides.
No kernel may reach another device: no remote copies, remote signals or barrier semaphores. Data moves between devices by JAX's collectives and lax.ppermute only.
A program may use at most 64 MiB of HBM per device.

```python
import math
import jax
import jax.numpy as jnp
from jax import lax

KBINS = 256
BX = 64
BY = 256
BZ = 8
NX = 256
NY = 512
NZ = 32
N_GX = 4
N_GY = 2
N_GZ = 4


def with_ends(result, own_key, least, largest):
    extent = result.shape
    place = [jax.random.randint(jax.random.fold_in(own_key, axis), (), 0, extent[axis]) for axis in range(len(extent))]
    result = result.at[tuple(place)].set(least)
    longest = extent.index(max(extent))
    place[longest] = (place[longest] + 1) % extent[longest]
    return result.at[tuple(place)].set(largest)


def levels(stream_key, shape, pieces, low, top_value):
    def one(position, shards_of):
        steps = jax.random.uniform(jax.random.fold_in(jax.random.fold_in(stream_key, 6), position), (shards_of,), jnp.float32, low / len(pieces), top_value / len(pieces))
        return jnp.repeat(jnp.exp(steps), shape[position] // shards_of).reshape((-1,) + (1,) * (len(shape) - position - 1))

    level = one(*pieces[0])
    for cut in pieces[1:]:
        level = level * one(*cut)
    return level


def setup_inputs(seed: int = 0) -> dict:
    key_of = jax.random.split(jax.random.key(seed), 6)
    return {
        "density": jnp.clip(jnp.exp(math.log(2.0) - 2.3025851 * jax.random.uniform(key_of[0], (NZ, NX, NY), jnp.float32) ** levels(key_of[0], (NZ, NX, NY), ((0, 4), (1, 4), (2, 2)), -0.2, 0.2)), 0.2, 2.0),
        "bins": with_ends(jax.random.randint(key_of[1], (NZ, NX, NY), 0, KBINS), jax.random.fold_in(key_of[1], 1), 0, KBINS - 1).astype(jnp.int32),
        "colour_table": jnp.clip(jax.random.uniform(key_of[2], (3, KBINS), jnp.float32, 0.049804688, 1.0), 0.049804688, 1.0).astype(jnp.bfloat16),
        "opacity_table": jnp.clip(jnp.exp(jax.random.uniform(key_of[3], (KBINS,), jnp.float32, math.log(0.19921875), math.log(2.5))), 0.19921875, 2.5).astype(jnp.bfloat16),
        "order": jax.vmap(lambda own: jax.random.permutation(own, N_GZ))(jax.random.split(key_of[4], N_GX * N_GY)).reshape((N_GX, N_GY, N_GZ)).astype(jnp.int32),
    }


def reference(density, bins, colour_table, opacity_table, order):
    padded = jnp.pad(density, 1)
    slope_depth = (padded[2:, 1:-1, 1:-1] - padded[:-2, 1:-1, 1:-1]) * 0.5
    slope_column = (padded[1:-1, 2:, 1:-1] - padded[1:-1, :-2, 1:-1]) * 0.5
    slope_row = (padded[1:-1, 1:-1, 2:] - padded[1:-1, 1:-1, :-2]) * 0.5
    facing = 0.64 * slope_depth + 0.48 * slope_column + 0.6 * slope_row
    length = jnp.sqrt(slope_depth * slope_depth + slope_column * slope_column + slope_row * slope_row + 1.0)
    shade = 0.25 + 0.75 * jnp.abs(facing) / length
    opacity = opacity_table.astype(jnp.float32)[bins]
    sigma = opacity * density * (3.0 / NZ)
    alpha = 1.0 - jnp.exp(-sigma)
    sigma_bricks = sigma.reshape(N_GZ, BZ, NX, NY)
    excl = jnp.cumsum(sigma_bricks, axis=1) - sigma_bricks
    weight = jnp.exp(-excl) * alpha.reshape(N_GZ, BZ, NX, NY) * shade.reshape(N_GZ, BZ, NX, NY)
    brick_depth = lax.optimization_barrier(jnp.sum(sigma_bricks, axis=1))
    earlier = (order[:, :, None, :] < order[:, :, :, None]).astype(jnp.float32)
    split_depth = brick_depth.reshape(N_GZ, N_GX, BX, N_GY, BY)
    prefix = jnp.einsum('uvab,buxvy->auxvy', earlier, split_depth, precision=lax.Precision.HIGHEST)
    attenuation = jnp.exp(-prefix.reshape(N_GZ, NX, NY))
    channels = []
    for channel in range(3):
        colour = colour_table[channel].astype(jnp.float32)[bins].reshape(N_GZ, BZ, NX, NY)
        brick_colour = lax.optimization_barrier(jnp.sum(weight * colour, axis=1))
        channels.append(lax.optimization_barrier(jnp.sum(attenuation * brick_colour, axis=0)))
    channels.append(1.0 - jnp.exp(-lax.optimization_barrier(jnp.sum(brick_depth, axis=0))))
    return jnp.stack(channels, axis=0)
```

```python
import functools
import math

import jax
import jax.numpy as jnp
from jax import lax
from jax.experimental import pallas as pl
from jax.experimental.pallas import tpu as pltpu
from jax.sharding import PartitionSpec as P

LANES = 128
SUBLANES = 8
VMEM = pl.BlockSpec(memory_space=pltpu.VMEM)
SMEM = pl.BlockSpec(memory_space=pltpu.SMEM)


def faces_kernel(even_ref, density_ref, z_a, z_b, x_a, x_b, y_a, y_b):
    depth, columns, rows = density_ref.shape
    even_x, even_y, even_z = (even_ref[i] == 1 for i in range(3))
    first, last = density_ref[0], density_ref[depth - 1]
    z_a[...] = jnp.where(even_z, last, first)
    z_b[...] = jnp.where(even_z, first, last)
    for z in range(depth):
        first, last = density_ref[z, 0:1, :], density_ref[z, columns - 1 : columns, :]
        x_a[z : z + 1, :] = jnp.where(even_x, last, first)
        x_b[z : z + 1, :] = jnp.where(even_x, first, last)
    lane = lax.broadcasted_iota(jnp.int32, (columns, LANES), 1)
    first = last = jnp.zeros((columns, LANES), jnp.float32)
    for z in range(depth):
        first = jnp.where(lane == z, pltpu.roll(density_ref[z, :, :LANES], z, 1), first)
        last = jnp.where(lane == z, pltpu.roll(density_ref[z, :, rows - LANES :], z + 1, 1), last)
    y_a[...] = jnp.where(even_y, last, first)
    y_b[...] = jnp.where(even_y, first, last)


def look(words, index, upper):
    low, high = (
        jnp.take_along_axis(half, index, axis=1, mode="promise_in_bounds") for half in words
    )
    return jnp.where(upper, high, low)


def brick_kernel(
    step, parts, scalar_ref, density_ref, bins_ref, colour_ref, opacity_ref, *refs
):
    (z_a, z_b, x_a, x_b, y_a, y_b), outs = refs[:6], refs[6:]
    depth, columns, rows = density_ref.shape
    even_x, even_y, even_z = (scalar_ref[i] == 1 for i in range(3))
    tiles = columns // SUBLANES
    per_part = tiles // parts

    colours = (colour_ref[...].astype(jnp.float32) * 4096.0).astype(jnp.int32)
    opacity = (opacity_ref[...].astype(jnp.float32) * 1024.0).astype(jnp.int32)
    red_green = colours[0:1] * 8192 + colours[1:2]
    blue_opacity = colours[2:3] * 8192 + opacity

    def halves(word):
        return [
            jnp.broadcast_to(word[:, i : i + LANES], (SUBLANES, LANES)) for i in (0, LANES)
        ]

    red_green, blue_opacity = halves(red_green), halves(blue_opacity)
    sub = lax.broadcasted_iota(jnp.int32, (SUBLANES, rows), 0)
    lane = lax.broadcasted_iota(jnp.int32, (SUBLANES, rows), 1)

    def one_tile(i, carry):
        part, within = i // per_part, i % per_part
        tile = scalar_ref[3 + part] * per_part + within
        x0 = pl.multiple_of(tile * SUBLANES, SUBLANES)
        here = pl.ds(x0, SUBLANES)
        above = pl.ds(pl.multiple_of(jnp.maximum(x0 - SUBLANES, 0), SUBLANES), SUBLANES)
        below = pl.ds(
            pl.multiple_of(jnp.minimum(x0 + SUBLANES, columns - SUBLANES), SUBLANES), SUBLANES
        )
        top, bottom = tile == 0, tile == tiles - 1
        plane = jnp.where(even_z, z_b[here, :], z_a[here, :])
        after = jnp.where(even_z, z_a[here, :], z_b[here, :])
        y_before = jnp.where(even_y, y_b[here, :], y_a[here, :])
        y_after = jnp.where(even_y, y_a[here, :], y_b[here, :])
        current = density_ref[0, here, :]
        total = jnp.zeros((SUBLANES, rows), jnp.float32)
        seen = jnp.ones((SUBLANES, rows), jnp.float32)
        sums = [jnp.zeros((SUBLANES, rows), jnp.float32) for _ in range(3)]
        for z in range(depth):
            following = density_ref[z + 1, here, :] if z + 1 < depth else after
            slope_depth = following - plane
            x_before = jnp.where(even_x, x_b[z : z + 1, :], x_a[z : z + 1, :])
            x_after = jnp.where(even_x, x_a[z : z + 1, :], x_b[z : z + 1, :])
            before = jnp.where(top, x_before, density_ref[z, above, :])
            beyond = jnp.where(bottom, x_after, density_ref[z, below, :])
            slope_column = pltpu.roll(
                jnp.where(sub == 0, beyond, current), SUBLANES - 1, 0
            ) - pltpu.roll(jnp.where(sub == SUBLANES - 1, before, current), 1, 0)
            slope_row = jnp.where(
                lane == rows - 1, y_after[:, z : z + 1], pltpu.roll(current, rows - 1, 1)
            ) - jnp.where(lane == 0, y_before[:, z : z + 1], pltpu.roll(current, 1, 1))
            facing = 0.32 * slope_depth + 0.24 * slope_column + 0.3 * slope_row
            square = (
                slope_depth * slope_depth + slope_column * slope_column + slope_row * slope_row
            )
            shade = 0.25 + 0.75 * jnp.abs(facing) * lax.rsqrt(0.25 * square + 1.0)
            bins = bins_ref[z, here, :]
            looked = []
            for c in range(0, rows, LANES):
                b = bins[:, c : c + LANES]
                index, upper = b & (LANES - 1), b >= LANES
                looked.append((look(red_green, index, upper), look(blue_opacity, index, upper)))
            rg, bo = (jnp.concatenate([v[i] for v in looked], axis=1) for i in range(2))
            opacity = (bo & 8191).astype(jnp.float32)
            total = total + opacity * current * step
            left = jnp.exp2(-total)
            weight = (seen - left) * shade
            seen = left
            entries = (rg >> 13, rg & 8191, bo >> 13)
            sums = [s + weight * e.astype(jnp.float32) for s, e in zip(sums, entries)]
            plane, current = current, following
        values = [s * (1.0 / 4096.0) for s in sums] + [total]
        for p in range(parts):

            @pl.when(part == p)
            def _():
                at = pl.ds(pl.multiple_of(within * SUBLANES, SUBLANES), SUBLANES)
                for c, v in enumerate(values):
                    outs[p][c, at, :] = v

        return carry

    lax.fori_loop(0, tiles, one_tile, 0)


def compose_kernel(count, scalar_ref, *refs):
    if len(refs) == 2:
        bricks, out = [refs[0].at[i] for i in range(count)], refs[1]
    else:
        bricks, out = refs[:count], refs[count]
    depths = [b[3] for b in bricks]
    sums = [jnp.zeros_like(depths[0]) for _ in range(3)]
    total = jnp.zeros_like(depths[0])
    for i, brick in enumerate(bricks):
        prefix = jnp.zeros_like(total)
        for j in range(count):
            if j != i:
                prefix = prefix + jnp.where(scalar_ref[j] < scalar_ref[i], depths[j], 0.0)
        left = jnp.exp2(-prefix)
        sums = [s + left * brick[c] for c, s in enumerate(sums)]
        total = total + depths[i]
    for c in range(3):
        out[c] = sums[c]
    out[3] = 1.0 - jnp.exp2(-total)


def swap(to_first, to_second, axis):
    n = lax.axis_size(axis)
    got = []
    for value, start in ((to_first, 0), (to_second, 1)):
        pairs = [(i, i + 1) for i in range(start, n - 1, 2)]
        if pairs:
            got.append(lax.ppermute(value, axis, pairs + [(j, i) for i, j in pairs]))
        else:
            got.append(jnp.zeros_like(value))
    return got


def local(density, bins, colour_table, opacity_table, order):
    depth, columns, rows = density.shape
    bricks = lax.axis_size("gz")
    me = lax.axis_index("gz")
    f32 = lambda *shape: jax.ShapeDtypeStruct(shape, jnp.float32)
    even = jnp.stack([1 - lax.axis_index(a) % 2 for a in ("gx", "gy", "gz")])
    faces = pl.pallas_call(
        faces_kernel,
        out_shape=[f32(columns, rows)] * 2 + [f32(depth, rows)] * 2 + [f32(columns, LANES)] * 2,
        in_specs=[SMEM, VMEM],
        out_specs=[VMEM] * 6,
        name="faces",
    )(even, density)
    z_a, z_b = swap(faces[0], faces[1], "gz")
    x_a, x_b = swap(faces[2], faces[3], "gx")
    y_a, y_b = swap(faces[4], faces[5], "gy")

    tile_rows = columns // bricks
    direct = tile_rows % SUBLANES == 0 and bricks & (bricks - 1) == 0
    parts = bricks if direct else 1
    owners = jnp.arange(parts, dtype=jnp.int32)
    if direct:
        owners = owners ^ me
    step = 3.0 / (depth * bricks) * math.log2(math.e) / 1024.0
    sent = pl.pallas_call(
        functools.partial(brick_kernel, step, parts),
        out_shape=[f32(4, columns // parts, rows)] * parts,
        in_specs=[SMEM] + [VMEM] * 10,
        out_specs=[VMEM] * parts,
        name="brick",
    )(
        jnp.concatenate([even, owners]), density, bins, colour_table, opacity_table[None, :],
        z_a, z_b, x_a, x_b, y_a, y_b,
    )
    ranks = order.reshape(-1)
    if direct:
        received = [sent[0]] + [
            lax.ppermute(sent[k], "gz", [(i, i ^ k) for i in range(bricks)])
            for k in range(1, bricks)
        ]
        ranks = ranks[owners]
    else:
        cut = jnp.moveaxis(sent[0].reshape(4, bricks, tile_rows, rows), 1, 0)
        received = [lax.all_to_all(cut, "gz", 0, 0)]
    return pl.pallas_call(
        functools.partial(compose_kernel, bricks),
        out_shape=f32(4, tile_rows, rows),
        in_specs=[SMEM] + [VMEM] * len(received),
        out_specs=VMEM,
        name="compose",
    )(ranks, *received)


def solution(mesh):
    return jax.shard_map(
        local,
        mesh=mesh,
        in_specs=(P("gz", "gx", "gy"), P("gz", "gx", "gy"), P(), P(), P("gx", "gy", None)),
        out_specs=P(None, ("gx", "gz"), "gy"),
        check_vma=False,
    )
```

```python
import functools
import math

import jax
import jax.numpy as jnp
from jax import lax
from jax.experimental import pallas as pl
from jax.experimental.pallas import tpu as pltpu
from jax.sharding import PartitionSpec as P

LANES = 128
SUBLANES = 8
VMEM = pl.BlockSpec(memory_space=pltpu.VMEM)
SMEM = pl.BlockSpec(memory_space=pltpu.SMEM)


def evens():
    return [lax.axis_index(axis) % 2 == 0 for axis in ("gx", "gy", "gz")]


def faces_kernel(density_ref, z_a, z_b, x_a, x_b, y_a, *y_b):
    depth, columns, rows = density_ref.shape
    even_x, even_y, even_z = evens()
    first, last = density_ref[0], density_ref[depth - 1]
    z_a[...] = jnp.where(even_z, last, first)
    z_b[...] = jnp.where(even_z, first, last)
    for z in range(depth):
        first, last = density_ref[z, 0:1, :], density_ref[z, columns - 1 : columns, :]
        x_a[z : z + 1, :] = jnp.where(even_x, last, first)
        x_b[z : z + 1, :] = jnp.where(even_x, first, last)
    lane = lax.broadcasted_iota(jnp.int32, (columns, LANES), 1)
    first = last = jnp.zeros((columns, LANES), jnp.float32)
    for z in range(depth):
        first = jnp.where(lane == z, pltpu.roll(density_ref[z, :, :LANES], z, 1), first)
        last = jnp.where(lane == z, pltpu.roll(density_ref[z, :, rows - LANES :], z + 1, 1), last)
    y_a[...] = jnp.where(even_y, last, first)
    for y in y_b:
        y[...] = jnp.where(even_y, first, last)


def look(words, index, upper):
    low, high = (
        jnp.take_along_axis(half, index, axis=1, mode="promise_in_bounds") for half in words
    )
    return jnp.where(upper, high, low)


def brick_kernel(
    step, parts, density_ref, bins_ref, colour_ref, opacity_ref, *refs
):
    halos, outs = refs[:-parts], refs[-parts:]
    z_a, z_b, x_a, x_b, y_a = halos[:5]
    depth, columns, rows = density_ref.shape
    even_x, even_y, even_z = evens()
    first_x, first_y, first_z = (lax.axis_index(a) == 0 for a in ("gx", "gy", "gz"))
    last_x, last_y, last_z = (
        lax.axis_index(a) == lax.axis_size(a) - 1 for a in ("gx", "gy", "gz")
    )
    me = lax.axis_index("gz")
    tiles = columns // SUBLANES
    per_part = tiles // parts

    colours = (colour_ref[...].astype(jnp.float32) * 4096.0).astype(jnp.int32)
    opacity = (opacity_ref[...].reshape(1, -1).astype(jnp.float32) * 1024.0).astype(jnp.int32)
    red_green = colours[0:1] * 8192 + colours[1:2]
    blue_opacity = colours[2:3] * 8192 + opacity

    def halves(word):
        return [
            jnp.broadcast_to(word[:, i : i + LANES], (SUBLANES, LANES)) for i in (0, LANES)
        ]

    red_green, blue_opacity = halves(red_green), halves(blue_opacity)
    sub = lax.broadcasted_iota(jnp.int32, (SUBLANES, rows), 0)
    lane = lax.broadcasted_iota(jnp.int32, (SUBLANES, rows), 1)

    def one_tile(i, carry):
        part, within = i // per_part, i % per_part
        tile = (part ^ me) * per_part + within if parts > 1 else i
        x0 = pl.multiple_of(tile * SUBLANES, SUBLANES)
        here = pl.ds(x0, SUBLANES)
        above = pl.ds(pl.multiple_of(jnp.maximum(x0 - SUBLANES, 0), SUBLANES), SUBLANES)
        below = pl.ds(
            pl.multiple_of(jnp.minimum(x0 + SUBLANES, columns - SUBLANES), SUBLANES), SUBLANES
        )
        top, bottom = tile == 0, tile == tiles - 1
        plane = jnp.where(first_z, 0.0, jnp.where(even_z, z_b[here, :], z_a[here, :]))
        after = jnp.where(last_z, 0.0, jnp.where(even_z, z_a[here, :], z_b[here, :]))
        y_before = y_after = y_a[here, :]
        if len(halos) == 6:
            y_before = jnp.where(even_y, halos[5][here, :], y_before)
            y_after = jnp.where(even_y, y_after, halos[5][here, :])
        y_before, y_after = jnp.where(first_y, 0.0, y_before), jnp.where(last_y, 0.0, y_after)
        current = density_ref[0, here, :]
        total = jnp.zeros((SUBLANES, rows), jnp.float32)
        seen = jnp.ones((SUBLANES, rows), jnp.float32)
        sums = [jnp.zeros((SUBLANES, rows), jnp.float32) for _ in range(3)]
        for z in range(depth):
            following = density_ref[z + 1, here, :] if z + 1 < depth else after
            slope_depth = following - plane
            x_before = jnp.where(even_x, x_b[z : z + 1, :], x_a[z : z + 1, :])
            x_before = jnp.where(first_x, 0.0, x_before)
            x_after = jnp.where(even_x, x_a[z : z + 1, :], x_b[z : z + 1, :])
            x_after = jnp.where(last_x, 0.0, x_after)
            before = jnp.where(top, x_before, density_ref[z, above, :])
            beyond = jnp.where(bottom, x_after, density_ref[z, below, :])
            slope_column = pltpu.roll(
                jnp.where(sub == 0, beyond, current), SUBLANES - 1, 0
            ) - pltpu.roll(jnp.where(sub == SUBLANES - 1, before, current), 1, 0)
            slope_row = jnp.where(
                lane == rows - 1, y_after[:, z : z + 1], pltpu.roll(current, rows - 1, 1)
            ) - jnp.where(lane == 0, y_before[:, z : z + 1], pltpu.roll(current, 1, 1))
            facing = 0.32 * slope_depth + 0.24 * slope_column + 0.3 * slope_row
            square = (
                slope_depth * slope_depth + slope_column * slope_column + slope_row * slope_row
            )
            shade = 0.25 + 0.75 * jnp.abs(facing) * lax.rsqrt(0.25 * square + 1.0)
            bins = bins_ref[z, here, :]
            looked = []
            for c in range(0, rows, LANES):
                b = bins[:, c : c + LANES]
                index, upper = b & (LANES - 1), b >= LANES
                looked.append((look(red_green, index, upper), look(blue_opacity, index, upper)))
            rg, bo = (jnp.concatenate([v[i] for v in looked], axis=1) for i in range(2))
            opacity = (bo & 8191).astype(jnp.float32)
            total = total + opacity * current * step
            left = jnp.exp2(-total)
            weight = (seen - left) * shade
            seen = left
            entries = (rg >> 13, rg & 8191, bo >> 13)
            sums = [s + weight * e.astype(jnp.float32) for s, e in zip(sums, entries)]
            plane, current = current, following
        values = [s * (1.0 / 4096.0) for s in sums] + [total]
        for p in range(parts):

            @pl.when(part == p)
            def _():
                at = pl.ds(pl.multiple_of(within * SUBLANES, SUBLANES), SUBLANES)
                for c, v in enumerate(values):
                    outs[p][c, at, :] = v

        return carry

    lax.fori_loop(0, tiles, one_tile, 0)


def compose_kernel(count, order_ref, *refs):
    if len(refs) == 2:
        bricks, out = [refs[0].at[i] for i in range(count)], refs[1]
        ranks = [order_ref[0, 0, i] for i in range(count)]
    else:
        bricks, out = refs[:count], refs[count]
        ranks = [order_ref[0, 0, lax.axis_index("gz") ^ i] for i in range(count)]
    depths = [b[3] for b in bricks]
    sums = [jnp.zeros_like(depths[0]) for _ in range(3)]
    total = jnp.zeros_like(depths[0])
    for i, brick in enumerate(bricks):
        prefix = jnp.zeros_like(total)
        for j in range(count):
            if j != i:
                prefix = prefix + jnp.where(ranks[j] < ranks[i], depths[j], 0.0)
        left = jnp.exp2(-prefix)
        sums = [s + left * brick[c] for c, s in enumerate(sums)]
        total = total + depths[i]
    for c in range(3):
        out[c] = sums[c]
    out[3] = 1.0 - jnp.exp2(-total)


AXES = ("gx", "gy", "gz")


def swap(values, axis):
    sizes = [lax.axis_size(a) for a in AXES]
    at, other = AXES.index(axis), 0 if axis != "gx" else 1
    strides = [sizes[1] * sizes[2], sizes[2], 1]
    got = []
    for start, value in enumerate(values):
        pairs = []
        for device in range(sizes[0] * sizes[1] * sizes[2]):
            where = [device // s % n for s, n in zip(strides, sizes)]
            partner = where[at] + 1 if where[at] % 2 == start else where[at] - 1
            if 0 <= partner < sizes[at]:
                where[at] = partner
            else:
                where[other] ^= 1
            pairs.append((device, sum(w * s for w, s in zip(where, strides))))
        got.append(lax.ppermute(value, AXES, pairs))
    return got


def local(density, bins, colour_table, opacity_table, order):
    depth, columns, rows = density.shape
    bricks = lax.axis_size("gz")
    near = lambda *shape: pltpu.VMEM(shape, jnp.float32)
    here = lambda *arrays: [pltpu.with_memory_space_constraint(a, pltpu.VMEM) for a in arrays]
    density, bins = here(density, bins)
    y_sides = 1 if lax.axis_size("gy") == 2 else 2
    faces = pl.pallas_call(
        faces_kernel,
        out_shape=[near(columns, rows)] * 2
        + [near(depth, rows)] * 2
        + [near(columns, LANES)] * y_sides,
        in_specs=[VMEM],
        out_specs=[VMEM] * (4 + y_sides),
        name="faces",
    )(density)
    halos = swap(faces[0:2], "gz") + swap(faces[2:4], "gx") + swap(faces[4:], "gy")

    tile_rows = columns // bricks
    direct = tile_rows % SUBLANES == 0 and bricks & (bricks - 1) == 0
    parts = bricks if direct else 1
    step = 3.0 / (depth * bricks) * math.log2(math.e) / 1024.0
    sent = pl.pallas_call(
        functools.partial(brick_kernel, step, parts),
        out_shape=[near(4, columns // parts, rows)] * parts,
        in_specs=[VMEM] * (4 + len(halos)),
        out_specs=[VMEM] * parts,
        name="brick",
    )(density, bins, colour_table, opacity_table, *here(*halos))
    if direct:
        received = [sent[0]] + [
            lax.ppermute(sent[k], "gz", [(i, i ^ k) for i in range(bricks)])
            for k in range(1, bricks)
        ]
    else:
        cut = jnp.moveaxis(sent[0].reshape(4, bricks, tile_rows, rows), 1, 0)
        received = [lax.all_to_all(cut, "gz", 0, 0)]
    return pl.pallas_call(
        functools.partial(compose_kernel, bricks),
        out_shape=jax.ShapeDtypeStruct((4, tile_rows, rows), jnp.float32),
        in_specs=[SMEM] + [VMEM] * len(received),
        out_specs=VMEM,
        name="compose",
    )(order, *here(*received))


def solution(mesh):
    return jax.shard_map(
        local,
        mesh=mesh,
        in_specs=(P("gz", "gx", "gy"), P("gz", "gx", "gy"), P(), P(), P("gx", "gy", None)),
        out_specs=P(None, ("gx", "gz"), "gy"),
        check_vma=False,
    )
```

```python
import functools
import math

import jax
import jax.numpy as jnp
from jax import lax
from jax.experimental import pallas as pl
from jax.experimental.pallas import tpu as pltpu
from jax.sharding import PartitionSpec as P

LANES = 128
SUBLANES = 8
AXES = ("gx", "gy", "gz")
SCOPED = 8 * 1024 * 1024
VMEM = pl.BlockSpec(memory_space=pltpu.VMEM)
HBM = pl.BlockSpec(memory_space=pltpu.HBM)


def evens():
    return [lax.axis_index(axis) % 2 == 0 for axis in AXES]


def ends():
    return [(lax.axis_index(a) == 0, lax.axis_index(a) == lax.axis_size(a) - 1) for a in AXES]


def load_kernel(density_hbm, order_hbm, colour_hbm, opacity_hbm, *refs):
    density_ref, order_ref, colour_ref, opacity_ref, z_a, z_b, x_a, x_b, y_a, *y_b, sems = refs
    depth, columns, rows = density_ref.shape
    even_x, even_y, even_z = evens()
    copies = [
        pltpu.make_async_copy(source, target, sems.at[i])
        for i, (source, target) in enumerate(
            (
                (density_hbm, density_ref),
                (order_hbm, order_ref),
                (colour_hbm, colour_ref),
                (opacity_hbm, opacity_ref),
            )
        )
    ]
    for copy in copies:
        copy.start()
    for copy in copies:
        copy.wait()
    first, last = density_ref[0], density_ref[depth - 1]
    z_a[...] = jnp.where(even_z, last, first)
    z_b[...] = jnp.where(even_z, first, last)
    for z in range(depth):
        first, last = density_ref[z, 0:1, :], density_ref[z, columns - 1 : columns, :]
        x_a[z : z + 1, :] = jnp.where(even_x, last, first)
        x_b[z : z + 1, :] = jnp.where(even_x, first, last)
    lane = lax.broadcasted_iota(jnp.int32, (columns, LANES), 1)
    first = last = jnp.zeros((columns, LANES), jnp.float32)
    for z in range(depth):
        first = jnp.where(lane == z, pltpu.roll(density_ref[z, :, :LANES], z, 1), first)
        last = jnp.where(lane == z, pltpu.roll(density_ref[z, :, rows - LANES :], z + 1, 1), last)
    y_a[...] = jnp.where(even_y, last, first)
    for y in y_b:
        y[...] = jnp.where(even_y, first, last)


def look(words, index, upper):
    low, high = (
        jnp.take_along_axis(half, index, axis=1, mode="promise_in_bounds") for half in words
    )
    return jnp.where(upper, high, low)


def pieces(rows):
    return [slice(c, c + LANES) for c in range(0, rows, LANES)]


def weights_kernel(
    step, relative, order_ref, density_ref, bins_hbm, colour_ref, opacity_ref,
    weighted, depth_out, earlier, bins_ref, sems,
):
    depth, columns, rows = density_ref.shape
    bricks = order_ref.shape[2]
    me = lax.axis_index("gz")

    def fetch(tile):
        at = pl.ds(pl.multiple_of(tile * SUBLANES, SUBLANES), SUBLANES)
        return pltpu.make_async_copy(
            bins_hbm.at[:, at, :], bins_ref.at[:, at, :], sems.at[tile]
        )

    lax.fori_loop(0, columns // SUBLANES, lambda i, c: fetch(i).start(), None)
    order = order_ref[0]
    brick = lax.broadcasted_iota(jnp.int32, order.shape, 1)
    ranks = [
        jnp.sum(jnp.where(brick == (i ^ me if relative else i), order, 0), axis=1, keepdims=True)
        for i in range(bricks)
    ]
    for i in range(bricks):
        for j in range(bricks):
            before = jnp.where(ranks[j] < ranks[i], 1.0, 0.0)
            earlier[i * bricks + j : i * bricks + j + 1, :] = jnp.broadcast_to(before, (1, rows))

    colours = (colour_ref[...].astype(jnp.float32) * 4096.0).astype(jnp.int32)
    opacity = (opacity_ref[...].reshape(1, -1).astype(jnp.float32) * 1024.0).astype(jnp.int32)
    red_green = colours[0:1] * 8192 + colours[1:2]
    blue_opacity = colours[2:3] * 8192 + opacity

    def halves(word):
        return [
            jnp.broadcast_to(word[:, i : i + LANES], (SUBLANES, LANES)) for i in (0, LANES)
        ]

    red_green, blue_opacity = halves(red_green), halves(blue_opacity)

    def one_tile(tile, carry):
        here = pl.ds(pl.multiple_of(tile * SUBLANES, SUBLANES), SUBLANES)
        fetch(tile).wait()
        for at in pieces(rows):
            total = jnp.zeros((SUBLANES, LANES), jnp.float32)
            seen = jnp.full((SUBLANES, LANES), 1.0 / 4096.0, jnp.float32)
            for z in range(depth):
                b = bins_ref[z, here, at]
                index, upper = b & (LANES - 1), b >= LANES
                rg, bo = look(red_green, index, upper), look(blue_opacity, index, upper)
                opacity = (bo & 8191).astype(jnp.float32)
                total = total + opacity * (density_ref[z, here, at] * step)
                left = jnp.exp2(-total) * (1.0 / 4096.0)
                weight = seen - left
                seen = left
                for c, entry in enumerate((rg >> 13, rg & 8191, bo >> 13)):
                    weighted[c, z, here, at] = weight * entry.astype(jnp.float32)
            depth_out[here, at] = total
        return carry

    lax.fori_loop(0, columns // SUBLANES, one_tile, 0)


def shade_kernel(part, density_ref, weighted, depth_in, *refs):
    halos, out, x_before, x_after = refs[:-3], refs[-3], refs[-2], refs[-1]
    z_a, z_b, x_a, x_b, y_a = halos[:5]
    depth, columns, rows = density_ref.shape
    even_x, even_y, even_z = evens()
    (first_x, last_x), (first_y, last_y), (first_z, last_z) = ends()
    tiles = out.shape[1] // SUBLANES
    start = 0 if part is None else (lax.axis_index("gz") ^ part) * tiles
    end = columns // SUBLANES - 1
    x_before[...] = jnp.where(first_x, 0.0, jnp.where(even_x, x_b[...], x_a[...]))
    x_after[...] = jnp.where(last_x, 0.0, jnp.where(even_x, x_a[...], x_b[...]))
    sub = lax.broadcasted_iota(jnp.int32, (SUBLANES, LANES), 0)
    lane = lax.broadcasted_iota(jnp.int32, (SUBLANES, LANES), 1)
    cuts = pieces(rows)

    def one_tile(i, carry):
        tile = start + i
        x0 = tile * SUBLANES
        here = pl.ds(pl.multiple_of(x0, SUBLANES), SUBLANES)
        above = pl.ds(pl.multiple_of(jnp.maximum(x0 - SUBLANES, 0), SUBLANES), SUBLANES)
        below = pl.ds(
            pl.multiple_of(jnp.minimum(x0 + SUBLANES, columns - SUBLANES), SUBLANES), SUBLANES
        )
        top, bottom = tile == 0, tile == end
        y_before = y_after = y_a[here, :]
        if len(halos) == 6:
            y_before = jnp.where(even_y, halos[5][here, :], y_before)
            y_after = jnp.where(even_y, y_after, halos[5][here, :])
        y_before, y_after = jnp.where(first_y, 0.0, y_before), jnp.where(last_y, 0.0, y_after)
        plane = [
            jnp.where(first_z, 0.0, jnp.where(even_z, z_b[here, at], z_a[here, at])) for at in cuts
        ]
        after = [
            jnp.where(last_z, 0.0, jnp.where(even_z, z_a[here, at], z_b[here, at])) for at in cuts
        ]
        current = [density_ref[0, here, at] for at in cuts]
        sums = [[jnp.zeros((SUBLANES, LANES), jnp.float32) for _ in range(3)] for _ in cuts]
        for z in range(depth):
            following = [density_ref[z + 1, here, at] for at in cuts] if z + 1 < depth else after
            right = [pltpu.roll(v, 1, 1) for v in current]
            left = [pltpu.roll(v, LANES - 1, 1) for v in current]
            for p, at in enumerate(cuts):
                low = right[p - 1] if p > 0 else y_before[:, z : z + 1]
                high = left[p + 1] if p + 1 < len(cuts) else y_after[:, z : z + 1]
                slope_row = jnp.where(lane == LANES - 1, high, left[p]) - jnp.where(
                    lane == 0, low, right[p]
                )
                before = jnp.where(top, x_before[z : z + 1, at], density_ref[z, above, at])
                beyond = jnp.where(bottom, x_after[z : z + 1, at], density_ref[z, below, at])
                slope_column = pltpu.roll(
                    jnp.where(sub == 0, beyond, current[p]), SUBLANES - 1, 0
                ) - pltpu.roll(jnp.where(sub == SUBLANES - 1, before, current[p]), 1, 0)
                slope_depth = following[p] - plane[p]
                facing = 0.48 * slope_depth + 0.36 * slope_column + 0.45 * slope_row
                square = (
                    slope_depth * slope_depth
                    + slope_column * slope_column
                    + (slope_row * slope_row + 4.0)
                )
                shade = 0.25 + jnp.abs(facing) * lax.rsqrt(square)
                for c in range(3):
                    sums[p][c] = sums[p][c] + shade * weighted[c, z, here, at]
            plane, current = current, following
        to = pl.ds(pl.multiple_of(i * SUBLANES, SUBLANES), SUBLANES)
        for p, at in enumerate(cuts):
            for c in range(3):
                out[c, to, at] = sums[p][c]
            out[3, to, at] = depth_in[here, at]
        return carry

    lax.fori_loop(0, tiles, one_tile, 0)


def compose_kernel(count, earlier, *refs):
    out = refs[-1]
    bricks = refs[count - 1 :: -1] if len(refs) > 2 else [refs[0].at[i] for i in range(count)]
    depths = [b[3] for b in bricks]
    sums = [jnp.zeros_like(depths[0]) for _ in range(3)]
    total = jnp.zeros_like(depths[0])
    for i, brick in enumerate(bricks):
        prefix = jnp.zeros_like(total)
        for j in range(count):
            if j != i:
                k = i * count + j
                prefix = prefix + earlier[k : k + 1, :] * depths[j]
        left = jnp.exp2(-prefix)
        sums = [s + left * brick[c] for c, s in enumerate(sums)]
        total = total + depths[i]
    for c in range(3):
        out[c] = sums[c]
    out[3] = 1.0 - jnp.exp2(-total)


def swap(values, axis):
    sizes = [lax.axis_size(a) for a in AXES]
    at, other = AXES.index(axis), 0 if axis != "gx" else 1
    strides = [sizes[1] * sizes[2], sizes[2], 1]
    got = []
    for start, value in enumerate(values):
        pairs = []
        for device in range(sizes[0] * sizes[1] * sizes[2]):
            where = [device // s % n for s, n in zip(strides, sizes)]
            partner = where[at] + 1 if where[at] % 2 == start else where[at] - 1
            if 0 <= partner < sizes[at]:
                where[at] = partner
            else:
                where[other] ^= 1
            pairs.append((device, sum(w * s for w, s in zip(where, strides))))
        got.append(lax.ppermute(value, AXES, pairs))
    return got


def local(density, bins, colour_table, opacity_table, order):
    depth, columns, rows = density.shape
    bricks = lax.axis_size("gz")
    near = lambda *shape: pltpu.VMEM(shape, jnp.float32)
    here = lambda *arrays: [pltpu.with_memory_space_constraint(a, pltpu.VMEM) for a in arrays]
    far = lambda *arrays: [pltpu.with_memory_space_constraint(a, pltpu.HBM) for a in arrays]
    call = lambda kernel, name, out_shape, in_specs, **more: pl.pallas_call(
        kernel, name=name, out_shape=out_shape, in_specs=in_specs,
        out_specs=jax.tree.map(lambda _: VMEM, out_shape),
        compiler_params=pltpu.CompilerParams(vmem_limit_bytes=SCOPED), **more,
    )
    y_sides = 1 if lax.axis_size("gy") == 2 else 2
    density, order, colour_table, opacity_table, *faces = call(
        load_kernel, "load",
        [pltpu.VMEM(a.shape, a.dtype) for a in (density, order, colour_table, opacity_table)]
        + [near(columns, rows)] * 2 + [near(depth, rows)] * 2 + [near(columns, LANES)] * y_sides,
        [HBM] * 4, scratch_shapes=[pltpu.SemaphoreType.DMA((4,))],
    )(*far(density, order, colour_table, opacity_table))
    density, order, colour_table, opacity_table, *faces = here(
        density, order, colour_table, opacity_table, *faces
    )
    halos = swap(faces[:2], "gz") + swap(faces[2:4], "gx") + swap(faces[4:], "gy")

    tile_rows = columns // bricks
    direct = tile_rows % SUBLANES == 0 and bricks & (bricks - 1) == 0
    step = 3.0 / (depth * bricks) * math.log2(math.e) / 1024.0
    weighted, depths, earlier = call(
        functools.partial(weights_kernel, step, direct), "weights",
        [near(3, depth, columns, rows), near(columns, rows), near(bricks * bricks, rows)],
        [VMEM] * 2 + [HBM] + [VMEM] * 2,
        scratch_shapes=[
            pltpu.VMEM(bins.shape, bins.dtype),
            pltpu.SemaphoreType.DMA((columns // SUBLANES,)),
        ],
    )(order, density, *far(bins), colour_table, opacity_table)
    weighted, depths, earlier = here(weighted, depths, earlier)
    shade = lambda part, tile: call(
        functools.partial(shade_kernel, part), "shade",
        near(4, tile, rows), [VMEM] * (3 + len(halos)),
        scratch_shapes=[pltpu.VMEM((depth, rows), jnp.float32)] * 2,
    )(density, weighted, depths, *here(*halos))
    if direct:
        received = []
        for k in range(bricks - 1, 0, -1):
            pairs = [(i, i ^ k) for i in range(bricks)]
            received.append(lax.ppermute(shade(k, tile_rows), "gz", pairs))
        received.append(shade(0, tile_rows))
    else:
        whole = shade(None, columns)
        cut = jnp.moveaxis(whole.reshape(4, bricks, tile_rows, rows), 1, 0)
        received = [lax.all_to_all(cut, "gz", 0, 0)]
    return call(
        functools.partial(compose_kernel, bricks), "compose",
        jax.ShapeDtypeStruct((4, tile_rows, rows), jnp.float32), [VMEM] * (1 + len(received)),
    )(earlier, *here(*received))


def solution(mesh):
    return jax.shard_map(
        local,
        mesh=mesh,
        in_specs=(P("gz", "gx", "gy"), P("gz", "gx", "gy"), P(), P(), P("gx", "gy", None)),
        out_specs=P(None, ("gx", "gz"), "gy"),
        check_vma=False,
    )
```

```python
import functools
import math

import jax
import jax.numpy as jnp
from jax import lax
from jax.experimental import pallas as pl
from jax.experimental.pallas import tpu as pltpu
from jax.sharding import PartitionSpec as P

LANES = 128
SUBLANES = 8
AXES = ("gx", "gy", "gz")
SCOPED = 8 * 1024 * 1024
VMEM = pl.BlockSpec(memory_space=pltpu.VMEM)
HBM = pl.BlockSpec(memory_space=pltpu.HBM)


def evens():
    return [lax.axis_index(axis) % 2 == 0 for axis in AXES]


def ends():
    return [(lax.axis_index(a) == 0, lax.axis_index(a) == lax.axis_size(a) - 1) for a in AXES]


def y_place(depth, tile):
    tiles = (LANES - 1) // depth
    return tile // tiles * SUBLANES, tile % tiles * depth


def y_shape(depth, columns):
    return y_place(depth, columns // SUBLANES - 1)[0] + SUBLANES, LANES


def depth_faces_kernel(density_ref, z_a, z_b, sems):
    last = density_ref.shape[0] - 1
    even = lax.axis_index("gz") % 2 == 0
    copies = [
        pltpu.make_async_copy(density_ref.at[jnp.where(even, last, 0)], z_a, sems.at[0]),
        pltpu.make_async_copy(density_ref.at[jnp.where(even, 0, last)], z_b.at[: z_a.shape[0]], sems.at[1]),
    ]
    for copy in copies:
        copy.start()
    for copy in copies:
        copy.wait()


def side_faces_kernel(density_ref, x_a, x_b, y_a, *y_b):
    depth, columns, rows = density_ref.shape
    even_x, even_y, _ = evens()
    odd_y = lax.axis_index("gy") % 2
    for out in (x_a, x_b, y_a, *y_b):
        out[...] = jnp.zeros_like(out)
    lane = lax.broadcasted_iota(jnp.int32, (SUBLANES, LANES), 1) - odd_y
    faces = {}
    for z in range(depth):
        first, last = density_ref[z, 0:1, :], density_ref[z, columns - 1 : columns, :]
        x_a[z : z + 1, :] = jnp.where(even_x, last, first)
        x_b[z : z + 1, :] = jnp.where(even_x, first, last)
        for tile in range(columns // SUBLANES):
            here = slice(tile * SUBLANES, (tile + 1) * SUBLANES)
            first, last = density_ref[z, here, :LANES], density_ref[z, here, rows - LANES :]
            to, at = y_place(depth, tile)
            for out, near_, far_ in ((y_a, last, first), *((y, first, last) for y in y_b)):
                edge = jnp.where(even_y, near_, far_)
                if out is not y_a:
                    edge = pltpu.roll(edge, jnp.where(even_y, LANES - 1, 1), 1)
                key = (to, out is y_a)
                faces[key] = jnp.where(
                    lane == at + z, pltpu.roll(edge, at + z + 1, 1), faces.get(key, 0.0)
                )
    for (to, is_a), value in faces.items():
        (y_a if is_a else y_b[0])[to : to + SUBLANES, :] = value


def look(words, index, upper):
    low, high = (
        jnp.take_along_axis(half, index, axis=1, mode="promise_in_bounds") for half in words
    )
    return jnp.where(upper, high, low)


def pieces(rows):
    return [slice(c, c + LANES) for c in range(0, rows, LANES)]


def weights_kernel(
    step, relative, order_ref, density_ref, bins_ref, colour_ref, opacity_ref,
    weighted, depth_out, earlier,
):
    depth, columns, rows = density_ref.shape
    bricks = order_ref.shape[2]
    me = lax.axis_index("gz")

    order = order_ref[0]
    brick = lax.broadcasted_iota(jnp.int32, order.shape, 1)
    ranks = [
        jnp.sum(jnp.where(brick == (i ^ me if relative else i), order, 0), axis=1, keepdims=True)
        for i in range(bricks)
    ]
    for i in range(bricks):
        for j in range(bricks):
            before = jnp.where(ranks[j] < ranks[i], 1.0, 0.0)
            earlier[i * bricks + j : i * bricks + j + 1, :] = jnp.broadcast_to(before, (1, rows))

    colours = (colour_ref[...].astype(jnp.float32) * 4096.0).astype(jnp.int32)
    opacity = (opacity_ref[...].reshape(1, -1).astype(jnp.float32) * 1024.0).astype(jnp.int32)
    red_green = colours[0:1] * 8192 + colours[1:2]
    blue_opacity = colours[2:3] * 8192 + opacity

    def halves(word):
        return [
            jnp.broadcast_to(word[:, i : i + LANES], (SUBLANES, LANES)) for i in (0, LANES)
        ]

    red_green, blue_opacity = halves(red_green), halves(blue_opacity)

    def one_tile(tile, carry):
        here = pl.ds(pl.multiple_of(tile * SUBLANES, SUBLANES), SUBLANES)
        for at in pieces(rows):
            total = jnp.zeros((SUBLANES, LANES), jnp.float32)
            seen = jnp.full((SUBLANES, LANES), 1.0 / 4096.0, jnp.float32)
            for z in range(depth):
                b = bins_ref[z, here, at]
                index, upper = b & (LANES - 1), b >= LANES
                rg, bo = look(red_green, index, upper), look(blue_opacity, index, upper)
                opacity = (bo & 8191).astype(jnp.float32)
                total = total + opacity * (density_ref[z, here, at] * step)
                left = jnp.exp2(-total) * (1.0 / 4096.0)
                weight = seen - left
                seen = left
                for c, entry in enumerate((rg >> 13, rg & 8191, bo >> 13)):
                    weighted[c, z, here, at] = weight * entry.astype(jnp.float32)
            depth_out[here, at] = total
        return carry

    lax.fori_loop(0, columns // SUBLANES, one_tile, 0, unroll=True)


def shade_kernel(part, density_ref, weighted, depth_in, *refs):
    halos, out, x_before, x_after = refs[:-3], refs[-3], refs[-2], refs[-1]
    z_a, z_b, x_a, x_b, y_a = halos[:5]
    depth, columns, rows = density_ref.shape
    even_x, even_y, even_z = evens()
    (first_x, last_x), (first_y, last_y), (first_z, last_z) = ends()
    tiles = out.shape[1] // SUBLANES
    start = 0 if part is None else (lax.axis_index("gz") ^ part) * tiles
    end = columns // SUBLANES - 1
    x_a, x_b = x_a[:depth, :], x_b[:depth, :]
    x_before[...] = jnp.where(first_x, 0.0, jnp.where(even_x, x_b, x_a))
    x_after[...] = jnp.where(last_x, 0.0, jnp.where(even_x, x_a, x_b))
    sub = lax.broadcasted_iota(jnp.int32, (SUBLANES, LANES), 0)
    lane = lax.broadcasted_iota(jnp.int32, (SUBLANES, LANES), 1)
    cuts = pieces(rows)

    def one_tile(i, carry):
        tile = start + i
        x0 = tile * SUBLANES
        here = pl.ds(pl.multiple_of(x0, SUBLANES), SUBLANES)
        above = pl.ds(pl.multiple_of(jnp.maximum(x0 - SUBLANES, 0), SUBLANES), SUBLANES)
        below = pl.ds(
            pl.multiple_of(jnp.minimum(x0 + SUBLANES, columns - SUBLANES), SUBLANES), SUBLANES
        )
        top, bottom = tile == 0, tile == end
        to, lane0 = y_place(depth, tile)
        turn = (LANES - lane0 - jnp.where(even_y, 1, 0)) % LANES
        y_rows = pl.ds(pl.multiple_of(to, SUBLANES), SUBLANES)
        y_before = y_after = pltpu.roll(y_a[y_rows, :], turn, 1)
        if len(halos) == 6:
            second = pltpu.roll(halos[5][y_rows, :], turn, 1)
            y_before = jnp.where(even_y, second, y_before)
            y_after = jnp.where(even_y, y_after, second)
        y_before, y_after = jnp.where(first_y, 0.0, y_before), jnp.where(last_y, 0.0, y_after)
        plane = [
            jnp.where(first_z, 0.0, jnp.where(even_z, z_b[here, at], z_a[here, at])) for at in cuts
        ]
        after = [
            jnp.where(last_z, 0.0, jnp.where(even_z, z_a[here, at], z_b[here, at])) for at in cuts
        ]
        current = [density_ref[0, here, at] for at in cuts]
        sums = [[jnp.zeros((SUBLANES, LANES), jnp.float32) for _ in range(3)] for _ in cuts]
        for z in range(depth):
            following = [density_ref[z + 1, here, at] for at in cuts] if z + 1 < depth else after
            right = [pltpu.roll(v, 1, 1) for v in current]
            left = [pltpu.roll(v, LANES - 1, 1) for v in current]
            for p, at in enumerate(cuts):
                low = right[p - 1] if p > 0 else y_before[:, z : z + 1]
                high = left[p + 1] if p + 1 < len(cuts) else y_after[:, z : z + 1]
                slope_row = jnp.where(lane == LANES - 1, high, left[p]) - jnp.where(
                    lane == 0, low, right[p]
                )
                before = jnp.where(top, x_before[z : z + 1, at], density_ref[z, above, at])
                beyond = jnp.where(bottom, x_after[z : z + 1, at], density_ref[z, below, at])
                slope_column = pltpu.roll(
                    jnp.where(sub == 0, beyond, current[p]), SUBLANES - 1, 0
                ) - pltpu.roll(jnp.where(sub == SUBLANES - 1, before, current[p]), 1, 0)
                slope_depth = following[p] - plane[p]
                facing = 0.48 * slope_depth + 0.36 * slope_column + 0.45 * slope_row
                square = (
                    slope_depth * slope_depth
                    + slope_column * slope_column
                    + (slope_row * slope_row + 4.0)
                )
                shade = 0.25 + jnp.abs(facing) * lax.rsqrt(square)
                for c in range(3):
                    sums[p][c] = sums[p][c] + shade * weighted[c, z, here, at]
            plane, current = current, following
        to = pl.ds(pl.multiple_of(i * SUBLANES, SUBLANES), SUBLANES)
        for p, at in enumerate(cuts):
            for c in range(3):
                out[c, to, at] = sums[p][c]
            out[3, to, at] = depth_in[here, at]
        return carry

    lax.fori_loop(0, tiles, one_tile, 0, unroll=tiles <= 2)


def compose_kernel(count, earlier, *refs):
    out = refs[-1]
    bricks = refs[count - 1 :: -1] if len(refs) > 2 else [refs[0].at[i] for i in range(count)]
    depths = [b[3] for b in bricks]
    sums = [jnp.zeros_like(depths[0]) for _ in range(3)]
    total = jnp.zeros_like(depths[0])
    for i, brick in enumerate(bricks):
        prefix = jnp.zeros_like(total)
        for j in range(count):
            if j != i:
                k = i * count + j
                prefix = prefix + earlier[k : k + 1, :] * depths[j]
        left = jnp.exp2(-prefix)
        sums = [s + left * brick[c] for c, s in enumerate(sums)]
        total = total + depths[i]
    for c in range(3):
        out[c] = sums[c]
    out[3] = 1.0 - jnp.exp2(-total)


def swap(values, axis):
    sizes = [lax.axis_size(a) for a in AXES]
    at, other = AXES.index(axis), 0
    strides = [sizes[1] * sizes[2], sizes[2], 1]
    got = []
    for start, value in enumerate(values):
        pairs = []
        for device in range(sizes[0] * sizes[1] * sizes[2]):
            where = [device // s % n for s, n in zip(strides, sizes)]
            partner = where[at] + 1 if where[at] % 2 == start else where[at] - 1
            if 0 <= partner < sizes[at]:
                where[at] = partner
            elif axis == "gx":
                where[at] = sizes[at] - 1 - where[at]
            else:
                where[other] ^= 1
            pairs.append((device, sum(w * s for w, s in zip(where, strides))))
        got.append(lax.ppermute(value, AXES, pairs))
    return got


def local(density, bins, colour_table, opacity_table, order):
    depth, columns, rows = density.shape
    bricks = lax.axis_size("gz")
    near = lambda *shape: pltpu.VMEM(shape, jnp.float32)
    here = lambda *arrays: [pltpu.with_memory_space_constraint(a, pltpu.VMEM) for a in arrays]
    far = lambda *arrays: [pltpu.with_memory_space_constraint(a, pltpu.HBM) for a in arrays]
    call = lambda kernel, name, out_shape, in_specs, **more: pl.pallas_call(
        kernel, name=name, out_shape=out_shape, in_specs=in_specs,
        out_specs=jax.tree.map(lambda _: VMEM, out_shape),
        compiler_params=pltpu.CompilerParams(vmem_limit_bytes=SCOPED), **more,
    )
    y_height, _ = y_shape(depth, columns)
    y_sides = 1 if lax.axis_size("gy") == 2 else 2
    z_faces = call(
        depth_faces_kernel, "depth_faces", [near(columns, rows), near(columns + SUBLANES, rows)], [HBM],
        scratch_shapes=[pltpu.SemaphoreType.DMA((2,))],
        cost_estimate=pl.CostEstimate(flops=2 * 10**9, bytes_accessed=2 * 10**6, transcendentals=0),
    )(*far(density))
    density, bins, order, colour_table, opacity_table = here(
        density, bins, order, colour_table, opacity_table
    )
    side_faces = call(
        side_faces_kernel, "side_faces",
        [near(depth, rows), near(2 * depth, rows)]
        + [near(y_height + 2 * SUBLANES, LANES)] * y_sides, [VMEM],
    )(density)
    faces = here(*z_faces, *side_faces)
    halos = swap(faces[:2], "gz") + swap(faces[2:4], "gx") + swap(faces[4:], "gy")

    tile_rows = columns // bricks
    direct = tile_rows % SUBLANES == 0 and bricks & (bricks - 1) == 0
    step = 3.0 / (depth * bricks) * math.log2(math.e) / 1024.0
    weighted, depths, earlier = call(
        functools.partial(weights_kernel, step, direct), "weights",
        [near(3, depth, columns, rows), near(columns, rows), near(bricks * bricks, rows)],
        [VMEM] * 5,
    )(order, density, bins, colour_table, opacity_table)
    weighted, depths, earlier = here(weighted, depths, earlier)
    shade = lambda part, tile: call(
        functools.partial(shade_kernel, part), "shade",
        near(4, tile, rows), [VMEM] * (3 + len(halos)),
        scratch_shapes=[pltpu.VMEM((depth, rows), jnp.float32)] * 2,
    )(density, weighted, depths, *here(*halos))
    if direct:
        received = []
        for k in range(bricks - 1, 0, -1):
            pairs = [(i, i ^ k) for i in range(bricks)]
            received.append(lax.ppermute(shade(k, tile_rows), "gz", pairs))
        received.append(shade(0, tile_rows))
    else:
        whole = shade(None, columns)
        cut = jnp.moveaxis(whole.reshape(4, bricks, tile_rows, rows), 1, 0)
        received = [lax.all_to_all(cut, "gz", 0, 0)]
    return call(
        functools.partial(compose_kernel, bricks), "compose",
        jax.ShapeDtypeStruct((4, tile_rows, rows), jnp.float32), [VMEM] * (1 + len(received)),
    )(earlier, *here(*received))


def solution(mesh):
    return jax.shard_map(
        local,
        mesh=mesh,
        in_specs=(P("gz", "gx", "gy"), P("gz", "gx", "gy"), P(), P(), P("gx", "gy", None)),
        out_specs=P(None, ("gx", "gz"), "gy"),
        check_vma=False,
    )
```

```python
import functools
import math

import jax
import jax.numpy as jnp
from jax import lax
from jax.experimental import pallas as pl
from jax.experimental.pallas import tpu as pltpu
from jax.sharding import PartitionSpec as P

LANES = 128
SUBLANES = 8
AXES = ("gx", "gy", "gz")
SCOPED = 8 * 1024 * 1024
VMEM = pl.BlockSpec(memory_space=pltpu.VMEM)
HBM = pl.BlockSpec(memory_space=pltpu.HBM)


def evens():
    return [lax.axis_index(axis) % 2 == 0 for axis in AXES]


def ends():
    return [(lax.axis_index(a) == 0, lax.axis_index(a) == lax.axis_size(a) - 1) for a in AXES]


def by_core(shift):
    even, odd = shift
    return even if even == odd else jnp.where(lax.axis_index("gx") % 2 == 0, even, odd)


def shifted(shift):
    nx, ny, nz = (lax.axis_size(a) for a in AXES)
    at = lambda x, y, z: (x * ny + y) * nz + z
    return [
        (at(x, y, z), at(x, y, (z + shift[x % 2]) % nz))
        for x in range(nx) for y in range(ny) for z in range(nz)
    ]


def y_place(depth, tile):
    tiles = (LANES - 1) // depth
    return tile // tiles * SUBLANES, tile % tiles * depth


def y_shape(depth, columns):
    return y_place(depth, columns // SUBLANES - 1)[0] + SUBLANES, LANES


def depth_faces_kernel(density_ref, z_a, z_b, sems):
    last = density_ref.shape[0] - 1
    even = lax.axis_index("gz") % 2 == 0
    copies = [
        pltpu.make_async_copy(density_ref.at[jnp.where(even, last, 0)], z_a, sems.at[0]),
        pltpu.make_async_copy(density_ref.at[jnp.where(even, 0, last)], z_b.at[: z_a.shape[0]], sems.at[1]),
    ]
    for copy in copies:
        copy.start()
    for copy in copies:
        copy.wait()


def side_faces_kernel(density_ref, x_a, x_b, y_a, *y_b):
    depth, columns, rows = density_ref.shape
    even_x, even_y, _ = evens()
    odd_y = lax.axis_index("gy") % 2
    for out in (x_a, x_b, y_a, *y_b):
        out[...] = jnp.zeros_like(out)
    lane = lax.broadcasted_iota(jnp.int32, (SUBLANES, LANES), 1) - odd_y
    faces = {}
    for z in range(depth):
        first, last = density_ref[z, 0:1, :], density_ref[z, columns - 1 : columns, :]
        x_a[z : z + 1, :] = jnp.where(even_x, last, first)
        x_b[z : z + 1, :] = jnp.where(even_x, first, last)
        for tile in range(columns // SUBLANES):
            here = slice(tile * SUBLANES, (tile + 1) * SUBLANES)
            first, last = density_ref[z, here, :LANES], density_ref[z, here, rows - LANES :]
            to, at = y_place(depth, tile)
            for out, near_, far_ in ((y_a, last, first), *((y, first, last) for y in y_b)):
                edge = jnp.where(even_y, near_, far_)
                if out is not y_a:
                    edge = pltpu.roll(edge, jnp.where(even_y, LANES - 1, 1), 1)
                key = (to, out is y_a)
                faces[key] = jnp.where(
                    lane == at + z, pltpu.roll(edge, at + z + 1, 1), faces.get(key, 0.0)
                )
    for (to, is_a), value in faces.items():
        (y_a if is_a else y_b[0])[to : to + SUBLANES, :] = value


def look(words, index, upper):
    low, high = (
        jnp.take_along_axis(half, index, axis=1, mode="promise_in_bounds") for half in words
    )
    return jnp.where(upper, high, low)


def pieces(rows):
    return [slice(c, c + LANES) for c in range(0, rows, LANES)]


def weights_kernel(
    step, shifts, order_ref, density_ref, bins_ref, colour_ref, opacity_ref,
    weighted, depth_out, earlier,
):
    depth, columns, rows = density_ref.shape
    bricks = order_ref.shape[2]
    me = lax.axis_index("gz")

    source = lambda i: i if shifts is None else (me + bricks - by_core(shifts[i])) % bricks
    order = order_ref[0]
    brick = lax.broadcasted_iota(jnp.int32, order.shape, 1)
    ranks = [
        jnp.sum(jnp.where(brick == source(i), order, 0), axis=1, keepdims=True)
        for i in range(bricks)
    ]
    for i in range(bricks):
        for j in range(bricks):
            before = jnp.where(ranks[j] < ranks[i], 1.0, 0.0)
            earlier[i * bricks + j : i * bricks + j + 1, :] = jnp.broadcast_to(before, (1, rows))

    colours = (colour_ref[...].astype(jnp.float32) * 4096.0).astype(jnp.int32)
    opacity = (opacity_ref[...].reshape(1, -1).astype(jnp.float32) * 1024.0).astype(jnp.int32)
    red_green = colours[0:1] * 8192 + colours[1:2]
    blue_opacity = colours[2:3] * 8192 + opacity

    def halves(word):
        return [
            jnp.broadcast_to(word[:, i : i + LANES], (SUBLANES, LANES)) for i in (0, LANES)
        ]

    red_green, blue_opacity = halves(red_green), halves(blue_opacity)

    def one_tile(tile, carry):
        here = pl.ds(pl.multiple_of(tile * SUBLANES, SUBLANES), SUBLANES)
        for at in pieces(rows):
            total = jnp.zeros((SUBLANES, LANES), jnp.float32)
            seen = jnp.full((SUBLANES, LANES), 1.0 / 4096.0, jnp.float32)
            for z in range(depth):
                b = bins_ref[z, here, at]
                index, upper = b & (LANES - 1), b >= LANES
                rg, bo = look(red_green, index, upper), look(blue_opacity, index, upper)
                opacity = (bo & 8191).astype(jnp.float32)
                total = total + opacity * (density_ref[z, here, at] * step)
                left = jnp.exp2(-total) * (1.0 / 4096.0)
                weight = seen - left
                seen = left
                for c, entry in enumerate((rg >> 13, rg & 8191, bo >> 13)):
                    weighted[c, z, here, at] = weight * entry.astype(jnp.float32)
            depth_out[here, at] = total
        return carry

    lax.fori_loop(0, columns // SUBLANES, one_tile, 0, unroll=True)


def shade_kernel(part, density_ref, weighted, depth_in, *refs):
    halos, out, x_before, x_after = refs[:-3], refs[-3], refs[-2], refs[-1]
    z_a, z_b, x_a, x_b, y_a = halos[:5]
    depth, columns, rows = density_ref.shape
    even_x, even_y, even_z = evens()
    (first_x, last_x), (first_y, last_y), (first_z, last_z) = ends()
    tiles = out.shape[1] // SUBLANES
    start = 0
    if part is not None:
        start = (lax.axis_index("gz") + by_core(part)) % lax.axis_size("gz") * tiles
    end = columns // SUBLANES - 1
    x_a, x_b = x_a[:depth, :], x_b[:depth, :]
    x_before[...] = jnp.where(first_x, 0.0, jnp.where(even_x, x_b, x_a))
    x_after[...] = jnp.where(last_x, 0.0, jnp.where(even_x, x_a, x_b))
    sub = lax.broadcasted_iota(jnp.int32, (SUBLANES, LANES), 0)
    lane = lax.broadcasted_iota(jnp.int32, (SUBLANES, LANES), 1)
    cuts = pieces(rows)

    def one_tile(i, carry):
        tile = start + i
        x0 = tile * SUBLANES
        here = pl.ds(pl.multiple_of(x0, SUBLANES), SUBLANES)
        above = pl.ds(pl.multiple_of(jnp.maximum(x0 - SUBLANES, 0), SUBLANES), SUBLANES)
        below = pl.ds(
            pl.multiple_of(jnp.minimum(x0 + SUBLANES, columns - SUBLANES), SUBLANES), SUBLANES
        )
        top, bottom = tile == 0, tile == end
        to, lane0 = y_place(depth, tile)
        turn = (LANES - lane0 - jnp.where(even_y, 1, 0)) % LANES
        y_rows = pl.ds(pl.multiple_of(to, SUBLANES), SUBLANES)
        y_before = y_after = pltpu.roll(y_a[y_rows, :], turn, 1)
        if len(halos) == 6:
            second = pltpu.roll(halos[5][y_rows, :], turn, 1)
            y_before = jnp.where(even_y, second, y_before)
            y_after = jnp.where(even_y, y_after, second)
        y_before, y_after = jnp.where(first_y, 0.0, y_before), jnp.where(last_y, 0.0, y_after)
        plane = [
            jnp.where(first_z, 0.0, jnp.where(even_z, z_b[here, at], z_a[here, at])) for at in cuts
        ]
        after = [
            jnp.where(last_z, 0.0, jnp.where(even_z, z_a[here, at], z_b[here, at])) for at in cuts
        ]
        current = [density_ref[0, here, at] for at in cuts]
        sums = [[jnp.zeros((SUBLANES, LANES), jnp.float32) for _ in range(3)] for _ in cuts]
        for z in range(depth):
            following = [density_ref[z + 1, here, at] for at in cuts] if z + 1 < depth else after
            right = [pltpu.roll(v, 1, 1) for v in current]
            left = [pltpu.roll(v, LANES - 1, 1) for v in current]
            for p, at in enumerate(cuts):
                low = right[p - 1] if p > 0 else y_before[:, z : z + 1]
                high = left[p + 1] if p + 1 < len(cuts) else y_after[:, z : z + 1]
                slope_row = jnp.where(lane == LANES - 1, high, left[p]) - jnp.where(
                    lane == 0, low, right[p]
                )
                before = jnp.where(top, x_before[z : z + 1, at], density_ref[z, above, at])
                beyond = jnp.where(bottom, x_after[z : z + 1, at], density_ref[z, below, at])
                slope_column = pltpu.roll(
                    jnp.where(sub == 0, beyond, current[p]), SUBLANES - 1, 0
                ) - pltpu.roll(jnp.where(sub == SUBLANES - 1, before, current[p]), 1, 0)
                slope_depth = following[p] - plane[p]
                facing = 0.48 * slope_depth + 0.36 * slope_column + 0.45 * slope_row
                square = (
                    slope_depth * slope_depth
                    + slope_column * slope_column
                    + (slope_row * slope_row + 4.0)
                )
                shade = 0.25 + jnp.abs(facing) * lax.rsqrt(square)
                for c in range(3):
                    sums[p][c] = sums[p][c] + shade * weighted[c, z, here, at]
            plane, current = current, following
        to = pl.ds(pl.multiple_of(i * SUBLANES, SUBLANES), SUBLANES)
        for p, at in enumerate(cuts):
            for c in range(3):
                out[c, to, at] = sums[p][c]
            out[3, to, at] = depth_in[here, at]
        return carry

    lax.fori_loop(0, tiles, one_tile, 0, unroll=tiles <= 2)


def compose_kernel(count, earlier, *refs):
    out = refs[-1]
    bricks = refs[:count] if len(refs) > 2 else [refs[0].at[i] for i in range(count)]
    depths = [b[3] for b in bricks]
    sums = [jnp.zeros_like(depths[0]) for _ in range(3)]
    total = jnp.zeros_like(depths[0])
    for i, brick in enumerate(bricks):
        prefix = jnp.zeros_like(total)
        for j in range(count):
            if j != i:
                k = i * count + j
                prefix = prefix + earlier[k : k + 1, :] * depths[j]
        left = jnp.exp2(-prefix)
        sums = [s + left * brick[c] for c, s in enumerate(sums)]
        total = total + depths[i]
    for c in range(3):
        out[c] = sums[c]
    out[3] = 1.0 - jnp.exp2(-total)


def swap(values, axis):
    sizes = [lax.axis_size(a) for a in AXES]
    at, other = AXES.index(axis), 0
    strides = [sizes[1] * sizes[2], sizes[2], 1]
    got = []
    for start, value in enumerate(values):
        pairs = []
        for device in range(sizes[0] * sizes[1] * sizes[2]):
            where = [device // s % n for s, n in zip(strides, sizes)]
            partner = where[at] + 1 if where[at] % 2 == start else where[at] - 1
            if 0 <= partner < sizes[at]:
                where[at] = partner
            elif axis == "gx":
                where[at] = sizes[at] - 1 - where[at]
            else:
                where[other] ^= 1
            pairs.append((device, sum(w * s for w, s in zip(where, strides))))
        got.append(lax.ppermute(value, AXES, pairs))
    return got


def local(density, bins, colour_table, opacity_table, order):
    depth, columns, rows = density.shape
    bricks = lax.axis_size("gz")
    near = lambda *shape: pltpu.VMEM(shape, jnp.float32)
    here = lambda *arrays: [pltpu.with_memory_space_constraint(a, pltpu.VMEM) for a in arrays]
    far = lambda *arrays: [pltpu.with_memory_space_constraint(a, pltpu.HBM) for a in arrays]
    call = lambda kernel, name, out_shape, in_specs, **more: pl.pallas_call(
        kernel, name=name, out_shape=out_shape, in_specs=in_specs,
        out_specs=jax.tree.map(lambda _: VMEM, out_shape),
        compiler_params=pltpu.CompilerParams(vmem_limit_bytes=SCOPED), **more,
    )
    y_height, _ = y_shape(depth, columns)
    y_sides = 1 if lax.axis_size("gy") == 2 else 2
    z_faces = call(
        depth_faces_kernel, "depth_faces", [near(columns, rows), near(columns + SUBLANES, rows)], [HBM],
        scratch_shapes=[pltpu.SemaphoreType.DMA((2,))],
        cost_estimate=pl.CostEstimate(flops=2 * 10**9, bytes_accessed=2 * 10**6, transcendentals=0),
    )(*far(density))
    density, bins, order, colour_table, opacity_table = here(
        density, bins, order, colour_table, opacity_table
    )
    side_faces = call(
        side_faces_kernel, "side_faces",
        [near(depth, rows), near(2 * depth, rows)]
        + [near(y_height + 2 * SUBLANES, LANES)] * y_sides, [VMEM],
    )(density)
    faces = here(*z_faces, *side_faces)
    halos = swap(faces[:2], "gz") + swap(faces[2:4], "gx") + swap(faces[4:], "gy")

    tile_rows = columns // bricks
    direct = tile_rows % SUBLANES == 0
    shifts = [(k, k % (bricks - 1) + 1) for k in range(1, bricks)] + [(0, 0)] if direct else None
    step = 3.0 / (depth * bricks) * math.log2(math.e) / 1024.0
    weighted, depths, earlier = call(
        functools.partial(weights_kernel, step, shifts), "weights",
        [near(3, depth, columns, rows), near(columns, rows), near(bricks * bricks, rows)],
        [VMEM] * 5,
    )(order, density, bins, colour_table, opacity_table)
    weighted, depths, earlier = here(weighted, depths, earlier)
    shade = lambda part, tile: call(
        functools.partial(shade_kernel, part), "shade",
        near(4, tile, rows), [VMEM] * (3 + len(halos)),
        scratch_shapes=[pltpu.VMEM((depth, rows), jnp.float32)] * 2,
    )(density, weighted, depths, *here(*halos))
    if direct:
        received = []
        for shift in shifts:
            part = shade(shift, tile_rows)
            if shift != (0, 0):
                part = lax.ppermute(part, AXES, shifted(shift))
            received.append(part)
    else:
        whole = shade(None, columns)
        cut = jnp.moveaxis(whole.reshape(4, bricks, tile_rows, rows), 1, 0)
        received = [lax.all_to_all(cut, "gz", 0, 0)]
    return call(
        functools.partial(compose_kernel, bricks), "compose",
        jax.ShapeDtypeStruct((4, tile_rows, rows), jnp.float32), [VMEM] * (1 + len(received)),
    )(earlier, *here(*received))


def solution(mesh):
    return jax.shard_map(
        local,
        mesh=mesh,
        in_specs=(P("gz", "gx", "gy"), P("gz", "gx", "gy"), P(), P(), P("gx", "gy", None)),
        out_specs=P(None, ("gx", "gz"), "gy"),
        check_vma=False,
    )
```

```python
import functools
import math

import jax
import jax.numpy as jnp
from jax import lax
from jax.experimental import pallas as pl
from jax.experimental.pallas import tpu as pltpu
from jax.sharding import PartitionSpec as P

LANES = 128
SUBLANES = 8
AXES = ("gx", "gy", "gz")
SCOPED = 8 * 1024 * 1024
VMEM = pl.BlockSpec(memory_space=pltpu.VMEM)
HBM = pl.BlockSpec(memory_space=pltpu.HBM)


def evens():
    return [lax.axis_index(axis) % 2 == 0 for axis in AXES]


def ends():
    return [(lax.axis_index(a) == 0, lax.axis_index(a) == lax.axis_size(a) - 1) for a in AXES]


def by_core(shift):
    even, odd = shift
    return even if even == odd else jnp.where(lax.axis_index("gx") % 2 == 0, even, odd)


def shifted(shift):
    nx, ny, nz = (lax.axis_size(a) for a in AXES)
    at = lambda x, y, z: (x * ny + y) * nz + z
    return [
        (at(x, y, z), at(x, y, (z + shift[x % 2]) % nz))
        for x in range(nx) for y in range(ny) for z in range(nz)
    ]


def y_place(depth, tile):
    tiles = (LANES - 1) // depth
    return tile // tiles * SUBLANES, tile % tiles * depth


def y_shape(depth, columns):
    return y_place(depth, columns // SUBLANES - 1)[0] + SUBLANES, LANES


def depth_faces_kernel(density_ref, z_a, z_b, sems):
    last = density_ref.shape[0] - 1
    even = lax.axis_index("gz") % 2 == 0
    half = density_ref.shape[1] // 2
    copies = []
    for out, plane in ((z_b, jnp.where(even, 0, last)), (z_a, jnp.where(even, last, 0))):
        for i in range(2):
            here = pl.ds(i * half, half)
            copies.append(
                pltpu.make_async_copy(density_ref.at[plane, here], out.at[here], sems.at[len(copies)])
            )
    for copy in copies:
        copy.start()
    for copy in copies:
        copy.wait()


def side_faces_kernel(density_ref, x_a, x_b, y_a, *y_b):
    depth, columns, rows = density_ref.shape
    even_x, even_y, _ = evens()
    odd_y = lax.axis_index("gy") % 2
    for out in (x_a, x_b, y_a, *y_b):
        out[...] = jnp.zeros_like(out)
    lane = lax.broadcasted_iota(jnp.int32, (SUBLANES, LANES), 1) - odd_y
    faces = {}
    for z in range(depth):
        first, last = density_ref[z, 0:1, :], density_ref[z, columns - 1 : columns, :]
        x_a[z : z + 1, :] = jnp.where(even_x, last, first)
        x_b[z : z + 1, :] = jnp.where(even_x, first, last)
        for tile in range(columns // SUBLANES):
            here = slice(tile * SUBLANES, (tile + 1) * SUBLANES)
            first, last = density_ref[z, here, :LANES], density_ref[z, here, rows - LANES :]
            to, at = y_place(depth, tile)
            for out, near_, far_ in ((y_a, last, first), *((y, first, last) for y in y_b)):
                edge = jnp.where(even_y, near_, far_)
                if out is not y_a:
                    edge = pltpu.roll(edge, jnp.where(even_y, LANES - 1, 1), 1)
                key = (to, out is y_a)
                faces[key] = jnp.where(
                    lane == at + z, pltpu.roll(edge, at + z + 1, 1), faces.get(key, 0.0)
                )
    for (to, is_a), value in faces.items():
        (y_a if is_a else y_b[0])[to : to + SUBLANES, :] = value


def look(words, index, upper):
    low, high = (
        jnp.take_along_axis(half, index, axis=1, mode="promise_in_bounds") for half in words
    )
    return jnp.where(upper, high, low)


def pieces(rows):
    return [slice(c, c + LANES) for c in range(0, rows, LANES)]


def weights_kernel(
    step, shifts, order_ref, density_ref, bins_ref, colour_ref, opacity_ref,
    weighted, depth_out, earlier,
):
    depth, columns, rows = density_ref.shape
    bricks = order_ref.shape[2]
    me = lax.axis_index("gz")

    source = lambda i: i if shifts is None else (me + bricks - by_core(shifts[i])) % bricks
    order = order_ref[0]
    brick = lax.broadcasted_iota(jnp.int32, order.shape, 1)
    ranks = [
        jnp.sum(jnp.where(brick == source(i), order, 0), axis=1, keepdims=True)
        for i in range(bricks)
    ]
    for i in range(bricks):
        for j in range(bricks):
            before = jnp.where(ranks[j] < ranks[i], 1.0, 0.0)
            earlier[i * bricks + j : i * bricks + j + 1, :] = jnp.broadcast_to(before, (1, rows))

    colours = (colour_ref[...].astype(jnp.float32) * 4096.0).astype(jnp.int32)
    opacity = (opacity_ref[...].reshape(1, -1).astype(jnp.float32) * 1024.0).astype(jnp.int32)
    red_green = colours[0:1] * 8192 + colours[1:2]
    blue_opacity = colours[2:3] * 8192 + opacity

    def halves(word):
        return [
            jnp.broadcast_to(word[:, i : i + LANES], (SUBLANES, LANES)) for i in (0, LANES)
        ]

    red_green, blue_opacity = halves(red_green), halves(blue_opacity)

    def one_tile(tile, carry):
        here = pl.ds(pl.multiple_of(tile * SUBLANES, SUBLANES), SUBLANES)
        for at in pieces(rows):
            total = jnp.zeros((SUBLANES, LANES), jnp.float32)
            seen = jnp.full((SUBLANES, LANES), 1.0 / 4096.0, jnp.float32)
            for z in range(depth):
                b = bins_ref[z, here, at]
                index, upper = b & (LANES - 1), b >= LANES
                rg, bo = look(red_green, index, upper), look(blue_opacity, index, upper)
                opacity = (bo & 8191).astype(jnp.float32)
                total = total + opacity * (density_ref[z, here, at] * step)
                left = jnp.exp2(-total) * (1.0 / 4096.0)
                weight = seen - left
                seen = left
                for c, entry in enumerate((rg >> 13, rg & 8191, bo >> 13)):
                    weighted[c, z, here, at] = weight * entry.astype(jnp.float32)
            depth_out[here, at] = total
        return carry

    lax.fori_loop(0, columns // SUBLANES, one_tile, 0, unroll=True)


def shade_kernel(part, density_ref, weighted, depth_in, *refs):
    halos, out, x_before, x_after = refs[:-3], refs[-3], refs[-2], refs[-1]
    z_a, z_b, x_a, x_b, y_a = halos[:5]
    depth, columns, rows = density_ref.shape
    even_x, even_y, even_z = evens()
    (first_x, last_x), (first_y, last_y), (first_z, last_z) = ends()
    tiles = out.shape[1] // SUBLANES
    start = 0
    if part is not None:
        start = (lax.axis_index("gz") + by_core(part)) % lax.axis_size("gz") * tiles
    end = columns // SUBLANES - 1
    x_a, x_b = x_a[:depth, :], x_b[:depth, :]
    x_before[...] = jnp.where(first_x, 0.0, jnp.where(even_x, x_b, x_a))
    x_after[...] = jnp.where(last_x, 0.0, jnp.where(even_x, x_a, x_b))
    sub = lax.broadcasted_iota(jnp.int32, (SUBLANES, LANES), 0)
    lane = lax.broadcasted_iota(jnp.int32, (SUBLANES, LANES), 1)
    cuts = pieces(rows)

    def one_tile(i, carry):
        tile = start + i
        x0 = tile * SUBLANES
        here = pl.ds(pl.multiple_of(x0, SUBLANES), SUBLANES)
        above = pl.ds(pl.multiple_of(jnp.maximum(x0 - SUBLANES, 0), SUBLANES), SUBLANES)
        below = pl.ds(
            pl.multiple_of(jnp.minimum(x0 + SUBLANES, columns - SUBLANES), SUBLANES), SUBLANES
        )
        top, bottom = tile == 0, tile == end
        to, lane0 = y_place(depth, tile)
        y_rows = pl.ds(pl.multiple_of(to, SUBLANES), SUBLANES)
        y_halos = [y[y_rows, :] for y in (y_a, *halos[5:])]
        y_lane = jnp.full((SUBLANES, LANES), lane0 + jnp.where(even_y, 1, 0), jnp.int32)
        plane = [
            jnp.where(first_z, 0.0, jnp.where(even_z, z_b[here, at], z_a[here, at])) for at in cuts
        ]
        after = [
            jnp.where(last_z, 0.0, jnp.where(even_z, z_a[here, at], z_b[here, at])) for at in cuts
        ]
        current = [density_ref[0, here, at] for at in cuts]
        sums = [[jnp.zeros((SUBLANES, LANES), jnp.float32) for _ in range(3)] for _ in cuts]
        for z in range(depth):
            following = [density_ref[z + 1, here, at] for at in cuts] if z + 1 < depth else after
            edges = [
                jnp.take_along_axis(y, y_lane + z, axis=1, mode="promise_in_bounds")
                for y in y_halos
            ]
            y_before = y_after = edges[0]
            if len(edges) == 2:
                y_before = jnp.where(even_y, edges[1], edges[0])
                y_after = jnp.where(even_y, edges[0], edges[1])
            y_before, y_after = jnp.where(first_y, 0.0, y_before), jnp.where(last_y, 0.0, y_after)
            right = [pltpu.roll(v, 1, 1) for v in current]
            left = [pltpu.roll(v, LANES - 1, 1) for v in current]
            for p, at in enumerate(cuts):
                low = right[p - 1] if p > 0 else y_before
                high = left[p + 1] if p + 1 < len(cuts) else y_after
                slope_row = jnp.where(lane == LANES - 1, high, left[p]) - jnp.where(
                    lane == 0, low, right[p]
                )
                before = jnp.where(top, x_before[z : z + 1, at], density_ref[z, above, at])
                beyond = jnp.where(bottom, x_after[z : z + 1, at], density_ref[z, below, at])
                slope_column = pltpu.roll(
                    jnp.where(sub == 0, beyond, current[p]), SUBLANES - 1, 0
                ) - pltpu.roll(jnp.where(sub == SUBLANES - 1, before, current[p]), 1, 0)
                slope_depth = following[p] - plane[p]
                facing = 0.48 * slope_depth + 0.36 * slope_column + 0.45 * slope_row
                square = (
                    slope_depth * slope_depth
                    + slope_column * slope_column
                    + (slope_row * slope_row + 4.0)
                )
                shade = 0.25 + jnp.abs(facing) * lax.rsqrt(square)
                for c in range(3):
                    sums[p][c] = sums[p][c] + shade * weighted[c, z, here, at]
            plane, current = current, following
        to = pl.ds(pl.multiple_of(i * SUBLANES, SUBLANES), SUBLANES)
        for p, at in enumerate(cuts):
            for c in range(3):
                out[c, to, at] = sums[p][c]
            out[3, to, at] = depth_in[here, at]
        return carry

    lax.fori_loop(0, tiles, one_tile, 0, unroll=tiles <= 2)


def compose_kernel(count, earlier, *refs):
    out = refs[-1]
    bricks = refs[:count] if len(refs) > 2 else [refs[0].at[i] for i in range(count)]
    depths = [b[3] for b in bricks]
    sums = [jnp.zeros_like(depths[0]) for _ in range(3)]
    total = jnp.zeros_like(depths[0])
    for i, brick in enumerate(bricks):
        prefix = jnp.zeros_like(total)
        for j in range(count):
            if j != i:
                k = i * count + j
                prefix = prefix + earlier[k : k + 1, :] * depths[j]
        left = jnp.exp2(-prefix)
        sums = [s + left * brick[c] for c, s in enumerate(sums)]
        total = total + depths[i]
    for c in range(3):
        out[c] = sums[c]
    out[3] = 1.0 - jnp.exp2(-total)


def swap(values, axis):
    sizes = [lax.axis_size(a) for a in AXES]
    at, other = AXES.index(axis), 0
    strides = [sizes[1] * sizes[2], sizes[2], 1]
    got = []
    for start, value in enumerate(values):
        pairs = []
        for device in range(sizes[0] * sizes[1] * sizes[2]):
            where = [device // s % n for s, n in zip(strides, sizes)]
            partner = where[at] + 1 if where[at] % 2 == start else where[at] - 1
            if 0 <= partner < sizes[at]:
                where[at] = partner
            elif axis == "gx":
                where[at] = sizes[at] - 1 - where[at]
            else:
                where[other] ^= 1
            pairs.append((device, sum(w * s for w, s in zip(where, strides))))
        got.append(lax.ppermute(value, AXES, pairs))
    return got


def local(density, bins, colour_table, opacity_table, order):
    depth, columns, rows = density.shape
    bricks = lax.axis_size("gz")
    near = lambda *shape: pltpu.VMEM(shape, jnp.float32)
    here = lambda *arrays: [pltpu.with_memory_space_constraint(a, pltpu.VMEM) for a in arrays]
    far = lambda *arrays: [pltpu.with_memory_space_constraint(a, pltpu.HBM) for a in arrays]
    call = lambda kernel, name, out_shape, in_specs, **more: pl.pallas_call(
        kernel, name=name, out_shape=out_shape, in_specs=in_specs,
        out_specs=jax.tree.map(lambda _: VMEM, out_shape),
        compiler_params=pltpu.CompilerParams(vmem_limit_bytes=SCOPED), **more,
    )
    y_height, _ = y_shape(depth, columns)
    y_sides = 1 if lax.axis_size("gy") == 2 else 2
    z_faces = call(
        depth_faces_kernel, "depth_faces", [near(columns, rows), near(columns + SUBLANES, rows)], [HBM],
        scratch_shapes=[pltpu.SemaphoreType.DMA((4,))],
        cost_estimate=pl.CostEstimate(flops=2 * 10**9, bytes_accessed=2 * 10**6, transcendentals=0),
    )(*far(density))
    density, bins, order, colour_table, opacity_table = here(
        density, bins, order, colour_table, opacity_table
    )
    side_faces = call(
        side_faces_kernel, "side_faces",
        [near(depth, rows), near(2 * depth, rows)]
        + [near(y_height + 2 * SUBLANES, LANES)] * y_sides, [VMEM],
    )(density)
    faces = here(*z_faces, *side_faces)
    halos = swap(faces[:2], "gz") + swap(faces[2:4], "gx") + swap(faces[4:], "gy")

    tile_rows = columns // bricks
    direct = tile_rows % SUBLANES == 0
    shifts = [(k, k % (bricks - 1) + 1) for k in range(1, bricks)] + [(0, 0)] if direct else None
    step = 3.0 / (depth * bricks) * math.log2(math.e) / 1024.0
    weighted, depths, earlier = call(
        functools.partial(weights_kernel, step, shifts), "weights",
        [near(3, depth, columns, rows), near(columns, rows), near(bricks * bricks, rows)],
        [VMEM] * 5,
    )(order, density, bins, colour_table, opacity_table)
    weighted, depths, earlier = here(weighted, depths, earlier)
    shade = lambda part, tile: call(
        functools.partial(shade_kernel, part), "shade",
        near(4, tile, rows), [VMEM] * (3 + len(halos)),
        scratch_shapes=[pltpu.VMEM((depth, rows), jnp.float32)] * 2,
    )(density, weighted, depths, *here(*halos))
    if direct:
        received = []
        for shift in shifts:
            part = shade(shift, tile_rows)
            if shift != (0, 0):
                part = lax.ppermute(part, AXES, shifted(shift))
            received.append(part)
    else:
        whole = shade(None, columns)
        cut = jnp.moveaxis(whole.reshape(4, bricks, tile_rows, rows), 1, 0)
        received = [lax.all_to_all(cut, "gz", 0, 0)]
    return call(
        functools.partial(compose_kernel, bricks), "compose",
        jax.ShapeDtypeStruct((4, tile_rows, rows), jnp.float32), [VMEM] * (1 + len(received)),
    )(earlier, *here(*received))


def solution(mesh):
    return jax.shard_map(
        local,
        mesh=mesh,
        in_specs=(P("gz", "gx", "gy"), P("gz", "gx", "gy"), P(), P(), P("gx", "gy", None)),
        out_specs=P(None, ("gx", "gz"), "gy"),
        check_vma=False,
    )
```

```python
import functools
import math

import jax
import jax.numpy as jnp
from jax import lax
from jax.experimental import pallas as pl
from jax.experimental.pallas import tpu as pltpu
from jax.sharding import PartitionSpec as P

LANES = 128
SUBLANES = 8
AXES = ("gx", "gy", "gz")
SCOPED = 8 * 1024 * 1024
VMEM = pl.BlockSpec(memory_space=pltpu.VMEM)
HBM = pl.BlockSpec(memory_space=pltpu.HBM)


def evens():
    return [lax.axis_index(axis) % 2 == 0 for axis in AXES]


def ends():
    return [(lax.axis_index(a) == 0, lax.axis_index(a) == lax.axis_size(a) - 1) for a in AXES]


def by_core(shift):
    even, odd = shift
    return even if even == odd else jnp.where(lax.axis_index("gx") % 2 == 0, even, odd)


def shifted(shift):
    nx, ny, nz = (lax.axis_size(a) for a in AXES)
    at = lambda x, y, z: (x * ny + y) * nz + z
    return [
        (at(x, y, z), at(x, y, (z + shift[x % 2]) % nz))
        for x in range(nx) for y in range(ny) for z in range(nz)
    ]


def y_place(depth, tile):
    tiles = (LANES - 1) // depth
    return tile // tiles * SUBLANES, tile % tiles * depth


def y_shape(depth, columns):
    return y_place(depth, columns // SUBLANES - 1)[0] + SUBLANES, LANES


def depth_faces_kernel(density_ref, z_a, z_b, sems):
    last = density_ref.shape[0] - 1
    even = lax.axis_index("gz") % 2 == 0
    half = density_ref.shape[1] // 2
    copies = []
    for out, plane in ((z_b, jnp.where(even, 0, last)), (z_a, jnp.where(even, last, 0))):
        for i in range(2):
            here = pl.ds(i * half, half)
            copies.append(
                pltpu.make_async_copy(density_ref.at[plane, here], out.at[here], sems.at[len(copies)])
            )
    for copy in copies:
        copy.start()
    for copy in copies:
        copy.wait()


def side_faces_kernel(density_ref, x_a, x_b, y_a, *y_b):
    depth, columns, rows = density_ref.shape
    even_x, even_y, _ = evens()
    odd_y = lax.axis_index("gy") % 2
    for out in (x_a, x_b, y_a, *y_b):
        out[...] = jnp.zeros_like(out)
    lane = lax.broadcasted_iota(jnp.int32, (SUBLANES, LANES), 1) - odd_y
    faces = {}
    for z in range(depth):
        first, last = density_ref[z, 0:1, :], density_ref[z, columns - 1 : columns, :]
        x_a[z : z + 1, :] = jnp.where(even_x, last, first)
        x_b[z : z + 1, :] = jnp.where(even_x, first, last)
        for tile in range(columns // SUBLANES):
            here = slice(tile * SUBLANES, (tile + 1) * SUBLANES)
            first, last = density_ref[z, here, :LANES], density_ref[z, here, rows - LANES :]
            to, at = y_place(depth, tile)
            for out, near_, far_ in ((y_a, last, first), *((y, first, last) for y in y_b)):
                edge = jnp.where(even_y, near_, far_)
                if out is not y_a:
                    edge = pltpu.roll(edge, jnp.where(even_y, LANES - 1, 1), 1)
                key = (to, out is y_a)
                faces[key] = jnp.where(
                    lane == at + z, pltpu.roll(edge, at + z + 1, 1), faces.get(key, 0.0)
                )
    for (to, is_a), value in faces.items():
        (y_a if is_a else y_b[0])[to : to + SUBLANES, :] = value


def look(words, index, upper):
    low, high = (
        jnp.take_along_axis(half, index, axis=1, mode="promise_in_bounds") for half in words
    )
    return jnp.where(upper, high, low)


def pieces(rows):
    return [slice(c, c + LANES) for c in range(0, rows, LANES)]


def weights_kernel(
    step, shifts, order_ref, density_ref, bins_ref, colour_ref, opacity_ref,
    weighted, depth_out, earlier,
):
    depth, columns, rows = density_ref.shape
    bricks = order_ref.shape[2]
    me = lax.axis_index("gz")

    source = lambda i: i if shifts is None else (me + bricks - by_core(shifts[i])) % bricks
    order = order_ref[0]
    brick = lax.broadcasted_iota(jnp.int32, order.shape, 1)
    ranks = [
        jnp.sum(jnp.where(brick == source(i), order, 0), axis=1, keepdims=True)
        for i in range(bricks)
    ]
    for i in range(bricks):
        for j in range(bricks):
            before = jnp.where(ranks[j] < ranks[i], 1.0, 0.0)
            earlier[i * bricks + j : i * bricks + j + 1, :] = jnp.broadcast_to(before, (1, rows))

    colours = (colour_ref[...].astype(jnp.float32) * 4096.0).astype(jnp.int32)
    opacity = (opacity_ref[...].reshape(1, -1).astype(jnp.float32) * 1024.0).astype(jnp.int32)
    red_green = colours[0:1] * 8192 + colours[1:2]
    blue_opacity = colours[2:3] * 8192 + opacity

    def halves(word):
        return [
            jnp.broadcast_to(word[:, i : i + LANES], (SUBLANES, LANES)) for i in (0, LANES)
        ]

    red_green, blue_opacity = halves(red_green), halves(blue_opacity)

    def one_tile(tile, carry):
        here = pl.ds(pl.multiple_of(tile * SUBLANES, SUBLANES), SUBLANES)
        for at in pieces(rows):
            total = jnp.zeros((SUBLANES, LANES), jnp.float32)
            seen = jnp.full((SUBLANES, LANES), 1.0 / 4096.0, jnp.float32)
            for z in range(depth):
                b = bins_ref[z, here, at]
                index, upper = b & (LANES - 1), b >= LANES
                rg, bo = look(red_green, index, upper), look(blue_opacity, index, upper)
                opacity = (bo & 8191).astype(jnp.float32)
                total = total + opacity * (density_ref[z, here, at] * step)
                left = jnp.exp2(-total) * (1.0 / 4096.0)
                weight = seen - left
                seen = left
                for c, entry in enumerate((rg >> 13, rg & 8191, bo >> 13)):
                    weighted[c, z, here, at] = weight * entry.astype(jnp.float32)
            depth_out[here, at] = total
        return carry

    lax.fori_loop(0, columns // SUBLANES, one_tile, 0, unroll=True)


def shade_kernel(part, density_ref, weighted, depth_in, *refs):
    halos, out, x_before, x_after = refs[:-3], refs[-3], refs[-2], refs[-1]
    z_a, z_b, *y_refs, x_a, x_b = halos
    depth, columns, rows = density_ref.shape
    even_x, even_y, even_z = evens()
    (first_x, last_x), (first_y, last_y), (first_z, last_z) = ends()
    tiles = out.shape[1] // SUBLANES
    start = 0
    if part is not None:
        start = (lax.axis_index("gz") + by_core(part)) % lax.axis_size("gz") * tiles
    end = columns // SUBLANES - 1
    x_a, x_b = x_a[:depth, :], x_b[:depth, :]
    x_before[...] = jnp.where(first_x, 0.0, jnp.where(even_x, x_b, x_a))
    x_after[...] = jnp.where(last_x, 0.0, jnp.where(even_x, x_a, x_b))
    sub = lax.broadcasted_iota(jnp.int32, (SUBLANES, LANES), 0)
    lane = lax.broadcasted_iota(jnp.int32, (SUBLANES, LANES), 1)
    cuts = pieces(rows)

    def one_tile(i, carry):
        tile = start + i
        x0 = tile * SUBLANES
        here = pl.ds(pl.multiple_of(x0, SUBLANES), SUBLANES)
        above = pl.ds(pl.multiple_of(jnp.maximum(x0 - SUBLANES, 0), SUBLANES), SUBLANES)
        below = pl.ds(
            pl.multiple_of(jnp.minimum(x0 + SUBLANES, columns - SUBLANES), SUBLANES), SUBLANES
        )
        top, bottom = tile == 0, tile == end
        to, lane0 = y_place(depth, tile)
        y_rows = pl.ds(pl.multiple_of(to, SUBLANES), SUBLANES)
        y_halos = [y[y_rows, :] for y in y_refs]
        y_lane = jnp.full((SUBLANES, LANES), lane0 + jnp.where(even_y, 1, 0), jnp.int32)
        plane = [
            jnp.where(first_z, 0.0, jnp.where(even_z, z_b[here, at], z_a[here, at])) for at in cuts
        ]
        after = [
            jnp.where(last_z, 0.0, jnp.where(even_z, z_a[here, at], z_b[here, at])) for at in cuts
        ]
        current = [density_ref[0, here, at] for at in cuts]
        sums = [[jnp.zeros((SUBLANES, LANES), jnp.float32) for _ in range(3)] for _ in cuts]
        for z in range(depth):
            following = [density_ref[z + 1, here, at] for at in cuts] if z + 1 < depth else after
            edges = [
                jnp.take_along_axis(y, y_lane + z, axis=1, mode="promise_in_bounds")
                for y in y_halos
            ]
            y_before = y_after = edges[0]
            if len(edges) == 2:
                y_before = jnp.where(even_y, edges[1], edges[0])
                y_after = jnp.where(even_y, edges[0], edges[1])
            y_before, y_after = jnp.where(first_y, 0.0, y_before), jnp.where(last_y, 0.0, y_after)
            right = [pltpu.roll(v, 1, 1) for v in current]
            left = [pltpu.roll(v, LANES - 1, 1) for v in current]
            for p, at in enumerate(cuts):
                low = right[p - 1] if p > 0 else y_before
                high = left[p + 1] if p + 1 < len(cuts) else y_after
                slope_row = jnp.where(lane == LANES - 1, high, left[p]) - jnp.where(
                    lane == 0, low, right[p]
                )
                before = jnp.where(top, x_before[z : z + 1, at], density_ref[z, above, at])
                beyond = jnp.where(bottom, x_after[z : z + 1, at], density_ref[z, below, at])
                slope_column = pltpu.roll(
                    jnp.where(sub == 0, beyond, current[p]), SUBLANES - 1, 0
                ) - pltpu.roll(jnp.where(sub == SUBLANES - 1, before, current[p]), 1, 0)
                slope_depth = following[p] - plane[p]
                facing = 0.48 * slope_depth + 0.36 * slope_column + 0.45 * slope_row
                square = (
                    slope_depth * slope_depth
                    + slope_column * slope_column
                    + (slope_row * slope_row + 4.0)
                )
                shade = 0.25 + jnp.abs(facing) * lax.rsqrt(square)
                for c in range(3):
                    sums[p][c] = sums[p][c] + shade * weighted[c, z, here, at]
            plane, current = current, following
        to = pl.ds(pl.multiple_of(i * SUBLANES, SUBLANES), SUBLANES)
        for p, at in enumerate(cuts):
            for c in range(3):
                out[c, to, at] = sums[p][c]
            out[3, to, at] = depth_in[here, at]
        return carry

    lax.fori_loop(0, tiles, one_tile, 0, unroll=tiles <= 2)


def compose_kernel(count, earlier, *refs):
    out = refs[-1]
    bricks = refs[:count] if len(refs) > 2 else [refs[0].at[i] for i in range(count)]
    depths = [b[3] for b in bricks]
    sums = [jnp.zeros_like(depths[0]) for _ in range(3)]
    total = jnp.zeros_like(depths[0])
    for i, brick in enumerate(bricks):
        prefix = jnp.zeros_like(total)
        for j in range(count):
            if j != i:
                k = i * count + j
                prefix = prefix + earlier[k : k + 1, :] * depths[j]
        left = jnp.exp2(-prefix)
        sums = [s + left * brick[c] for c, s in enumerate(sums)]
        total = total + depths[i]
    for c in range(3):
        out[c] = sums[c]
    out[3] = 1.0 - jnp.exp2(-total)


def swap(values, axis):
    sizes = [lax.axis_size(a) for a in AXES]
    at, other = AXES.index(axis), 0
    strides = [sizes[1] * sizes[2], sizes[2], 1]
    got = []
    for start, value in enumerate(values):
        pairs = []
        for device in range(sizes[0] * sizes[1] * sizes[2]):
            where = [device // s % n for s, n in zip(strides, sizes)]
            partner = where[at] + 1 if where[at] % 2 == start else where[at] - 1
            if 0 <= partner < sizes[at]:
                where[at] = partner
            elif axis == "gx":
                where[at] = sizes[at] - 1 - where[at]
            else:
                where[other] ^= 1
            pairs.append((device, sum(w * s for w, s in zip(where, strides))))
        got.append(lax.ppermute(value, AXES, pairs))
    return got


def local(density, bins, colour_table, opacity_table, order):
    depth, columns, rows = density.shape
    bricks = lax.axis_size("gz")
    near = lambda *shape: pltpu.VMEM(shape, jnp.float32)
    here = lambda *arrays: [pltpu.with_memory_space_constraint(a, pltpu.VMEM) for a in arrays]
    far = lambda *arrays: [pltpu.with_memory_space_constraint(a, pltpu.HBM) for a in arrays]
    call = lambda kernel, name, out_shape, in_specs, **more: pl.pallas_call(
        kernel, name=name, out_shape=out_shape, in_specs=in_specs,
        out_specs=jax.tree.map(lambda _: VMEM, out_shape),
        compiler_params=pltpu.CompilerParams(vmem_limit_bytes=SCOPED), **more,
    )
    y_height, _ = y_shape(depth, columns)
    y_sides = 1 if lax.axis_size("gy") == 2 else 2
    z_faces = call(
        depth_faces_kernel, "depth_faces", [near(columns + SUBLANES, rows), near(columns, rows)], [HBM],
        scratch_shapes=[pltpu.SemaphoreType.DMA((4,))],
        cost_estimate=pl.CostEstimate(flops=2 * 10**9, bytes_accessed=2 * 10**6, transcendentals=0),
    )(*far(density))
    density, bins, order, colour_table, opacity_table = here(
        density, bins, order, colour_table, opacity_table
    )
    side_faces = call(
        side_faces_kernel, "side_faces",
        [near(depth, rows), near(2 * depth, rows)]
        + [near(y_height + SUBLANES, LANES)] * y_sides, [VMEM],
        cost_estimate=pl.CostEstimate(flops=7 * 10**8, bytes_accessed=2 * 10**6, transcendentals=0),

    )(density)
    faces = here(*z_faces, *side_faces)
    halos = swap(faces[:2], "gz") + swap(faces[4:], "gy") + swap(faces[2:4], "gx")

    tile_rows = columns // bricks
    direct = tile_rows % SUBLANES == 0
    shifts = [(k, k % (bricks - 1) + 1) for k in range(1, bricks)] + [(0, 0)] if direct else None
    step = 3.0 / (depth * bricks) * math.log2(math.e) / 1024.0
    weighted, depths, earlier = call(
        functools.partial(weights_kernel, step, shifts), "weights",
        [near(3, depth, columns, rows), near(columns, rows), near(bricks * bricks, rows)],
        [VMEM] * 5,
    )(order, density, bins, colour_table, opacity_table)
    weighted, depths, earlier = here(weighted, depths, earlier)
    shade = lambda part, tile: call(
        functools.partial(shade_kernel, part), "shade",
        near(4, tile, rows), [VMEM] * (3 + len(halos)),
        scratch_shapes=[pltpu.VMEM((depth, rows), jnp.float32)] * 2,
    )(density, weighted, depths, *here(*halos))
    if direct:
        received = []
        for shift in shifts:
            part = shade(shift, tile_rows)
            if shift != (0, 0):
                part = lax.ppermute(part, AXES, shifted(shift))
            received.append(part)
    else:
        whole = shade(None, columns)
        cut = jnp.moveaxis(whole.reshape(4, bricks, tile_rows, rows), 1, 0)
        received = [lax.all_to_all(cut, "gz", 0, 0)]
    return call(
        functools.partial(compose_kernel, bricks), "compose",
        jax.ShapeDtypeStruct((4, tile_rows, rows), jnp.float32), [VMEM] * (1 + len(received)),
    )(earlier, *here(*received))


def solution(mesh):
    return jax.shard_map(
        local,
        mesh=mesh,
        in_specs=(P("gz", "gx", "gy"), P("gz", "gx", "gy"), P(), P(), P("gx", "gy", None)),
        out_specs=P(None, ("gx", "gz"), "gy"),
        check_vma=False,
    )
```

```python
import functools
import math

import jax
import jax.numpy as jnp
from jax import lax
from jax.experimental import pallas as pl
from jax.experimental.pallas import tpu as pltpu
from jax.sharding import PartitionSpec as P

LANES = 128
SUBLANES = 8
AXES = ("gx", "gy", "gz")
SCOPED = 8 * 1024 * 1024
VMEM = pl.BlockSpec(memory_space=pltpu.VMEM)
HBM = pl.BlockSpec(memory_space=pltpu.HBM)


def evens():
    return [lax.axis_index(axis) % 2 == 0 for axis in AXES]


def ends():
    return [(lax.axis_index(a) == 0, lax.axis_index(a) == lax.axis_size(a) - 1) for a in AXES]


def by_core(shift):
    even, odd = shift
    return even if even == odd else jnp.where(lax.axis_index("gx") % 2 == 0, even, odd)


def shifted(shift):
    nx, ny, nz = (lax.axis_size(a) for a in AXES)
    at = lambda x, y, z: (x * ny + y) * nz + z
    return [
        (at(x, y, z), at(x, y, (z + shift[x % 2]) % nz))
        for x in range(nx) for y in range(ny) for z in range(nz)
    ]


def y_place(depth, tile):
    tiles = (LANES - 1) // depth
    return tile // tiles * SUBLANES, tile % tiles * depth


def y_shape(depth, columns):
    return y_place(depth, columns // SUBLANES - 1)[0] + SUBLANES, LANES


def depth_faces_kernel(density_ref, z_a, z_b, sems):
    last = density_ref.shape[0] - 1
    even = lax.axis_index("gz") % 2 == 0
    half = density_ref.shape[1] // 2
    copies = []
    for out, plane in ((z_b, jnp.where(even, 0, last)), (z_a, jnp.where(even, last, 0))):
        for i in range(2):
            here = pl.ds(i * half, half)
            copies.append(
                pltpu.make_async_copy(density_ref.at[plane, here], out.at[here], sems.at[len(copies)])
            )
    for copy in copies:
        copy.start()
    for copy in copies:
        copy.wait()


def side_faces_kernel(density_ref, x_a, x_b, y_a, *y_b):
    depth, columns, rows = density_ref.shape
    even_x, even_y, _ = evens()
    odd_y = lax.axis_index("gy") % 2
    for out in (x_a, x_b, y_a, *y_b):
        out[...] = jnp.zeros_like(out)
    lane = lax.broadcasted_iota(jnp.int32, (SUBLANES, LANES), 1) - odd_y
    faces = {}
    for z in range(depth):
        first, last = density_ref[z, 0:1, :], density_ref[z, columns - 1 : columns, :]
        x_a[z : z + 1, :] = jnp.where(even_x, last, first)
        x_b[z : z + 1, :] = jnp.where(even_x, first, last)
        for tile in range(columns // SUBLANES):
            here = slice(tile * SUBLANES, (tile + 1) * SUBLANES)
            first, last = density_ref[z, here, :LANES], density_ref[z, here, rows - LANES :]
            to, at = y_place(depth, tile)
            for out, near_, far_ in ((y_a, last, first), *((y, first, last) for y in y_b)):
                edge = jnp.where(even_y, near_, far_)
                if out is not y_a:
                    edge = pltpu.roll(edge, jnp.where(even_y, LANES - 1, 1), 1)
                key = (to, out is y_a)
                faces[key] = jnp.where(
                    lane == at + z, pltpu.roll(edge, at + z + 1, 1), faces.get(key, 0.0)
                )
    for (to, is_a), value in faces.items():
        (y_a if is_a else y_b[0])[to : to + SUBLANES, :] = value


def look(words, index, upper):
    low, high = (
        jnp.take_along_axis(half, index, axis=1, mode="promise_in_bounds") for half in words
    )
    return jnp.where(upper, high, low)


def pieces(rows):
    return [slice(c, c + LANES) for c in range(0, rows, LANES)]


def weights_kernel(
    step, shifts, order_ref, density_ref, bins_ref, colour_ref, opacity_ref,
    weighted, depth_out, earlier,
):
    depth, columns, rows = density_ref.shape
    bricks = order_ref.shape[2]
    me = lax.axis_index("gz")

    source = lambda i: i if shifts is None else (me + bricks - by_core(shifts[i])) % bricks
    order = order_ref[0]
    brick = lax.broadcasted_iota(jnp.int32, order.shape, 1)
    ranks = [
        jnp.sum(jnp.where(brick == source(i), order, 0), axis=1, keepdims=True)
        for i in range(bricks)
    ]
    for i in range(bricks):
        for j in range(bricks):
            before = jnp.where(ranks[j] < ranks[i], 1.0, 0.0)
            earlier[i * bricks + j : i * bricks + j + 1, :] = jnp.broadcast_to(before, (1, rows))

    colours = (colour_ref[...].astype(jnp.float32) * 4096.0).astype(jnp.int32)
    powers = sum((colours >= 256 << i).astype(jnp.int32) for i in range(5))
    codes = powers * 128 + (jnp.right_shift(colours, powers) - 128)
    opacity = (opacity_ref[...].reshape(1, -1).astype(jnp.float32) * 1024.0).astype(jnp.int32)
    every = lambda word: jnp.broadcast_to(word, (SUBLANES, LANES))
    colour_word = codes[0:1] * 1048576 + codes[1:2] * 1024 + codes[2:3]
    colour_word = [every(colour_word[:, i : i + LANES]) for i in (0, LANES)]
    opacity_word = every(opacity[:, LANES:] * 4096 + opacity[:, :LANES])

    def one_tile(tile, carry):
        here = pl.ds(pl.multiple_of(tile * SUBLANES, SUBLANES), SUBLANES)
        for at in pieces(rows):
            total = jnp.zeros((SUBLANES, LANES), jnp.float32)
            seen = jnp.full((SUBLANES, LANES), 1.0 / 4096.0, jnp.float32)
            for z in range(depth):
                b = bins_ref[z, here, at]
                index, upper = b & (LANES - 1), b >= LANES
                colour = look(colour_word, index, upper)
                both = jnp.take_along_axis(opacity_word, index, axis=1, mode="promise_in_bounds")
                opacity = jnp.where(upper, both >> 12, both & 4095).astype(jnp.float32)
                total = total + opacity * (density_ref[z, here, at] * step)
                left = jnp.exp2(-total) * (1.0 / 4096.0)
                weight = seen - left
                seen = left
                for c in range(3):
                    code = (colour >> (20 - 10 * c)) & 1023
                    entry = jnp.left_shift((code & 127) + 128, code >> 7)
                    weighted[c, z, here, at] = weight * entry.astype(jnp.float32)
            depth_out[here, at] = total
        return carry

    lax.fori_loop(0, columns // SUBLANES, one_tile, 0, unroll=True)


def shade_kernel(part, density_ref, weighted, depth_in, *refs):
    halos, out, x_before, x_after = refs[:-3], refs[-3], refs[-2], refs[-1]
    z_a, z_b, *y_refs, x_a, x_b = halos
    depth, columns, rows = density_ref.shape
    even_x, even_y, even_z = evens()
    (first_x, last_x), (first_y, last_y), (first_z, last_z) = ends()
    tiles = out.shape[1] // SUBLANES
    start = 0
    if part is not None:
        start = (lax.axis_index("gz") + by_core(part)) % lax.axis_size("gz") * tiles
    end = columns // SUBLANES - 1
    x_a, x_b = x_a[:depth, :], x_b[:depth, :]
    x_before[...] = jnp.where(first_x, 0.0, jnp.where(even_x, x_b, x_a))
    x_after[...] = jnp.where(last_x, 0.0, jnp.where(even_x, x_a, x_b))
    sub = lax.broadcasted_iota(jnp.int32, (SUBLANES, LANES), 0)
    lane = lax.broadcasted_iota(jnp.int32, (SUBLANES, LANES), 1)
    cuts = pieces(rows)

    def one_tile(i, carry):
        tile = start + i
        x0 = tile * SUBLANES
        here = pl.ds(pl.multiple_of(x0, SUBLANES), SUBLANES)
        above = pl.ds(pl.multiple_of(jnp.maximum(x0 - SUBLANES, 0), SUBLANES), SUBLANES)
        below = pl.ds(
            pl.multiple_of(jnp.minimum(x0 + SUBLANES, columns - SUBLANES), SUBLANES), SUBLANES
        )
        top, bottom = tile == 0, tile == end
        to, lane0 = y_place(depth, tile)
        y_rows = pl.ds(pl.multiple_of(to, SUBLANES), SUBLANES)
        y_halos = [y[y_rows, :] for y in y_refs]
        y_lane = jnp.full((SUBLANES, LANES), lane0 + jnp.where(even_y, 1, 0), jnp.int32)
        plane = [
            jnp.where(first_z, 0.0, jnp.where(even_z, z_b[here, at], z_a[here, at])) for at in cuts
        ]
        after = [
            jnp.where(last_z, 0.0, jnp.where(even_z, z_a[here, at], z_b[here, at])) for at in cuts
        ]
        current = [density_ref[0, here, at] for at in cuts]
        sums = [[jnp.zeros((SUBLANES, LANES), jnp.float32) for _ in range(3)] for _ in cuts]
        for z in range(depth):
            following = [density_ref[z + 1, here, at] for at in cuts] if z + 1 < depth else after
            edges = [
                jnp.take_along_axis(y, y_lane + z, axis=1, mode="promise_in_bounds")
                for y in y_halos
            ]
            y_before = y_after = edges[0]
            if len(edges) == 2:
                y_before = jnp.where(even_y, edges[1], edges[0])
                y_after = jnp.where(even_y, edges[0], edges[1])
            y_before, y_after = jnp.where(first_y, 0.0, y_before), jnp.where(last_y, 0.0, y_after)
            right = [pltpu.roll(v, 1, 1) for v in current]
            left = [pltpu.roll(v, LANES - 1, 1) for v in current]
            for p, at in enumerate(cuts):
                low = right[p - 1] if p > 0 else y_before
                high = left[p + 1] if p + 1 < len(cuts) else y_after
                slope_row = jnp.where(lane == LANES - 1, high, left[p]) - jnp.where(
                    lane == 0, low, right[p]
                )
                before = jnp.where(top, x_before[z : z + 1, at], density_ref[z, above, at])
                beyond = jnp.where(bottom, x_after[z : z + 1, at], density_ref[z, below, at])
                slope_column = pltpu.roll(
                    jnp.where(sub == 0, beyond, current[p]), SUBLANES - 1, 0
                ) - pltpu.roll(jnp.where(sub == SUBLANES - 1, before, current[p]), 1, 0)
                slope_depth = following[p] - plane[p]
                facing = 0.48 * slope_depth + 0.36 * slope_column + 0.45 * slope_row
                square = (
                    slope_depth * slope_depth
                    + slope_column * slope_column
                    + (slope_row * slope_row + 4.0)
                )
                shade = 0.25 + jnp.abs(facing) * lax.rsqrt(square)
                for c in range(3):
                    sums[p][c] = sums[p][c] + shade * weighted[c, z, here, at]
            plane, current = current, following
        to = pl.ds(pl.multiple_of(i * SUBLANES, SUBLANES), SUBLANES)
        for p, at in enumerate(cuts):
            for c in range(3):
                out[c, to, at] = sums[p][c]
            out[3, to, at] = depth_in[here, at]
        return carry

    lax.fori_loop(0, tiles, one_tile, 0, unroll=tiles <= 2)


def compose_kernel(count, earlier, *refs):
    out = refs[-1]
    bricks = refs[:count] if len(refs) > 2 else [refs[0].at[i] for i in range(count)]
    depths = [b[3] for b in bricks]
    sums = [jnp.zeros_like(depths[0]) for _ in range(3)]
    total = jnp.zeros_like(depths[0])
    for i, brick in enumerate(bricks):
        prefix = jnp.zeros_like(total)
        for j in range(count):
            if j != i:
                k = i * count + j
                prefix = prefix + earlier[k : k + 1, :] * depths[j]
        left = jnp.exp2(-prefix)
        sums = [s + left * brick[c] for c, s in enumerate(sums)]
        total = total + depths[i]
    for c in range(3):
        out[c] = sums[c]
    out[3] = 1.0 - jnp.exp2(-total)


def swap(values, axis):
    sizes = [lax.axis_size(a) for a in AXES]
    at, other = AXES.index(axis), 0
    strides = [sizes[1] * sizes[2], sizes[2], 1]
    got = []
    for start, value in enumerate(values):
        pairs = []
        for device in range(sizes[0] * sizes[1] * sizes[2]):
            where = [device // s % n for s, n in zip(strides, sizes)]
            partner = where[at] + 1 if where[at] % 2 == start else where[at] - 1
            if 0 <= partner < sizes[at]:
                where[at] = partner
            elif axis == "gx":
                where[at] = sizes[at] - 1 - where[at]
            else:
                where[other] ^= 1
            pairs.append((device, sum(w * s for w, s in zip(where, strides))))
        got.append(lax.ppermute(value, AXES, pairs))
    return got


def local(density, bins, colour_table, opacity_table, order):
    depth, columns, rows = density.shape
    bricks = lax.axis_size("gz")
    near = lambda *shape: pltpu.VMEM(shape, jnp.float32)
    here = lambda *arrays: [pltpu.with_memory_space_constraint(a, pltpu.VMEM) for a in arrays]
    far = lambda *arrays: [pltpu.with_memory_space_constraint(a, pltpu.HBM) for a in arrays]
    call = lambda kernel, name, out_shape, in_specs, **more: pl.pallas_call(
        kernel, name=name, out_shape=out_shape, in_specs=in_specs,
        out_specs=jax.tree.map(lambda _: VMEM, out_shape),
        compiler_params=pltpu.CompilerParams(vmem_limit_bytes=SCOPED), **more,
    )
    y_height, _ = y_shape(depth, columns)
    y_sides = 1 if lax.axis_size("gy") == 2 else 2
    z_faces = call(
        depth_faces_kernel, "depth_faces", [near(columns + SUBLANES, rows), near(columns, rows)], [HBM],
        scratch_shapes=[pltpu.SemaphoreType.DMA((4,))],
        cost_estimate=pl.CostEstimate(flops=2 * 10**9, bytes_accessed=2 * 10**6, transcendentals=0),
    )(*far(density))
    density, bins, order, colour_table, opacity_table = here(
        density, bins, order, colour_table, opacity_table
    )
    side_faces = call(
        side_faces_kernel, "side_faces",
        [near(depth, rows), near(2 * depth, rows)]
        + [near(y_height + SUBLANES, LANES)] * y_sides, [VMEM],
        cost_estimate=pl.CostEstimate(flops=7 * 10**8, bytes_accessed=2 * 10**6, transcendentals=0),

    )(density)
    faces = here(*z_faces, *side_faces)
    halos = swap(faces[:2], "gz") + swap(faces[4:], "gy") + swap(faces[2:4], "gx")

    tile_rows = columns // bricks
    direct = tile_rows % SUBLANES == 0
    shifts = [(k, k % (bricks - 1) + 1) for k in range(1, bricks)] + [(0, 0)] if direct else None
    step = 3.0 / (depth * bricks) * math.log2(math.e) / 1024.0
    weighted, depths, earlier = call(
        functools.partial(weights_kernel, step, shifts), "weights",
        [near(3, depth, columns, rows), near(columns, rows), near(bricks * bricks, rows)],
        [VMEM] * 5,
    )(order, density, bins, colour_table, opacity_table)
    weighted, depths, earlier = here(weighted, depths, earlier)
    shade = lambda part, tile: call(
        functools.partial(shade_kernel, part), "shade",
        near(4, tile, rows), [VMEM] * (3 + len(halos)),
        scratch_shapes=[pltpu.VMEM((depth, rows), jnp.float32)] * 2,
    )(density, weighted, depths, *here(*halos))
    if direct:
        received = []
        for shift in shifts:
            part = shade(shift, tile_rows)
            if shift != (0, 0):
                part = lax.ppermute(part, AXES, shifted(shift))
            received.append(part)
    else:
        whole = shade(None, columns)
        cut = jnp.moveaxis(whole.reshape(4, bricks, tile_rows, rows), 1, 0)
        received = [lax.all_to_all(cut, "gz", 0, 0)]
    return call(
        functools.partial(compose_kernel, bricks), "compose",
        jax.ShapeDtypeStruct((4, tile_rows, rows), jnp.float32), [VMEM] * (1 + len(received)),
    )(earlier, *here(*received))


def solution(mesh):
    return jax.shard_map(
        local,
        mesh=mesh,
        in_specs=(P("gz", "gx", "gy"), P("gz", "gx", "gy"), P(), P(), P("gx", "gy", None)),
        out_specs=P(None, ("gx", "gz"), "gy"),
        check_vma=False,
    )
```

```python
import functools
import math

import jax
import jax.numpy as jnp
from jax import lax
from jax.experimental import pallas as pl
from jax.experimental.pallas import tpu as pltpu
from jax.sharding import PartitionSpec as P

LANES = 128
SUBLANES = 8
AXES = ("gx", "gy", "gz")
SCOPED = 8 * 1024 * 1024
VMEM = pl.BlockSpec(memory_space=pltpu.VMEM)
HBM = pl.BlockSpec(memory_space=pltpu.HBM)


def evens():
    return [lax.axis_index(axis) % 2 == 0 for axis in AXES]


def ends():
    return [(lax.axis_index(a) == 0, lax.axis_index(a) == lax.axis_size(a) - 1) for a in AXES]


def by_core(shift):
    even, odd = shift
    return even if even == odd else jnp.where(lax.axis_index("gx") % 2 == 0, even, odd)


def shifted(shift):
    nx, ny, nz = (lax.axis_size(a) for a in AXES)
    at = lambda x, y, z: (x * ny + y) * nz + z
    return [
        (at(x, y, z), at(x, y, (z + shift[x % 2]) % nz))
        for x in range(nx) for y in range(ny) for z in range(nz)
    ]


def y_place(depth, tile):
    tiles = (LANES - 1) // depth
    return tile // tiles * SUBLANES, tile % tiles * depth


def y_shape(depth, columns):
    return y_place(depth, columns // SUBLANES - 1)[0] + SUBLANES, LANES


def depth_faces_kernel(density_ref, z_a, z_b, sems):
    last = density_ref.shape[0] - 1
    even = lax.axis_index("gz") % 2 == 0
    half = density_ref.shape[1] // 2
    copies = []
    for out, plane in ((z_b, jnp.where(even, 0, last)), (z_a, jnp.where(even, last, 0))):
        for i in range(2):
            here = pl.ds(i * half, half)
            copies.append(
                pltpu.make_async_copy(density_ref.at[plane, here], out.at[here], sems.at[len(copies)])
            )
    for copy in copies:
        copy.start()
    for copy in copies:
        copy.wait()


def side_faces_kernel(density_ref, x_a, x_b, y_a, *y_b):
    depth, columns, rows = density_ref.shape
    even_x, even_y, _ = evens()
    odd_y = lax.axis_index("gy") % 2
    for out in (x_a, x_b, y_a, *y_b):
        out[...] = jnp.zeros_like(out)
    lane = lax.broadcasted_iota(jnp.int32, (SUBLANES, LANES), 1) - odd_y
    starts = [jnp.where(even_y, rows - LANES, 0), jnp.where(even_y, 0, rows - LANES)]
    faces = {}
    for z in range(depth):
        first, last = density_ref[z, 0:1, :], density_ref[z, columns - 1 : columns, :]
        x_a[z : z + 1, :] = jnp.where(even_x, last, first)
        x_b[z : z + 1, :] = jnp.where(even_x, first, last)
        for tile in range(columns // SUBLANES):
            here = slice(tile * SUBLANES, (tile + 1) * SUBLANES)
            to, at = y_place(depth, tile)
            for out, start in zip((y_a, *y_b), starts):
                edge = density_ref[z, here, pl.ds(pl.multiple_of(start, LANES), LANES)]
                if out is not y_a:
                    edge = pltpu.roll(edge, jnp.where(even_y, LANES - 1, 1), 1)
                key = (to, out is y_a)
                faces[key] = jnp.where(
                    lane == at + z, pltpu.roll(edge, at + z + 1, 1), faces.get(key, 0.0)
                )
    for (to, is_a), value in faces.items():
        (y_a if is_a else y_b[0])[to : to + SUBLANES, :] = value


def look(words, index, upper):
    low, high = (
        jnp.take_along_axis(half, index, axis=1, mode="promise_in_bounds") for half in words
    )
    return jnp.where(upper, high, low)


def pieces(rows):
    return [slice(c, c + LANES) for c in range(0, rows, LANES)]


def weights_kernel(
    step, shifts, order_ref, density_ref, bins_ref, colour_ref, opacity_ref,
    weighted, depth_out, earlier,
):
    depth, columns, rows = density_ref.shape
    bricks = order_ref.shape[2]
    me = lax.axis_index("gz")

    source = lambda i: i if shifts is None else (me + bricks - by_core(shifts[i])) % bricks
    order = order_ref[0]
    brick = lax.broadcasted_iota(jnp.int32, order.shape, 1)
    ranks = [
        jnp.sum(jnp.where(brick == source(i), order, 0), axis=1, keepdims=True)
        for i in range(bricks)
    ]
    for i in range(bricks):
        for j in range(bricks):
            before = jnp.where(ranks[j] < ranks[i], 1.0, 0.0)
            earlier[i * bricks + j : i * bricks + j + 1, :] = jnp.broadcast_to(before, (1, rows))

    colours = (colour_ref[...].astype(jnp.float32) * 4096.0).astype(jnp.int32)
    powers = sum((colours >= 256 << i).astype(jnp.int32) for i in range(5))
    codes = powers * 128 + (jnp.right_shift(colours, powers) - 128)
    opacity = (opacity_ref[...].reshape(1, -1).astype(jnp.float32) * 1024.0).astype(jnp.int32)
    every = lambda word: jnp.broadcast_to(word, (SUBLANES, LANES))
    colour_word = codes[0:1] * 1048576 + codes[1:2] * 1024 + codes[2:3]
    colour_word = [every(colour_word[:, i : i + LANES]) for i in (0, LANES)]
    opacity_word = every(opacity[:, LANES:] * 4096 + opacity[:, :LANES])

    def one_tile(tile, carry):
        here = pl.ds(pl.multiple_of(tile * SUBLANES, SUBLANES), SUBLANES)
        for at in pieces(rows):
            total = jnp.zeros((SUBLANES, LANES), jnp.float32)
            seen = jnp.full((SUBLANES, LANES), 1.0 / 4096.0, jnp.float32)
            for z in range(depth):
                b = bins_ref[z, here, at]
                index, upper = b & (LANES - 1), b >= LANES
                colour = look(colour_word, index, upper)
                both = jnp.take_along_axis(opacity_word, index, axis=1, mode="promise_in_bounds")
                opacity = jnp.where(upper, both >> 12, both & 4095).astype(jnp.float32)
                total = total + opacity * (density_ref[z, here, at] * step)
                left = jnp.exp2(-total) * (1.0 / 4096.0)
                weight = seen - left
                seen = left
                for c in range(3):
                    code = (colour >> (20 - 10 * c)) & 1023
                    entry = jnp.left_shift((code & 127) + 128, code >> 7)
                    weighted[c, z, here, at] = weight * entry.astype(jnp.float32)
            depth_out[here, at] = total
        return carry

    lax.fori_loop(0, columns // SUBLANES, one_tile, 0, unroll=True)


def shade_kernel(part, density_ref, weighted, depth_in, *refs):
    halos, out, x_before, x_after = refs[:-3], refs[-3], refs[-2], refs[-1]
    z_a, z_b, *y_refs, x_a, x_b = halos
    depth, columns, rows = density_ref.shape
    even_x, even_y, even_z = evens()
    (first_x, last_x), (first_y, last_y), (first_z, last_z) = ends()
    tiles = out.shape[1] // SUBLANES
    start = 0
    if part is not None:
        start = (lax.axis_index("gz") + by_core(part)) % lax.axis_size("gz") * tiles
    end = columns // SUBLANES - 1
    x_a, x_b = x_a[:depth, :], x_b[:depth, :]
    x_before[...] = jnp.where(first_x, 0.0, jnp.where(even_x, x_b, x_a))
    x_after[...] = jnp.where(last_x, 0.0, jnp.where(even_x, x_a, x_b))
    sub = lax.broadcasted_iota(jnp.int32, (SUBLANES, LANES), 0)
    lane = lax.broadcasted_iota(jnp.int32, (SUBLANES, LANES), 1)
    cuts = pieces(rows)

    def one_tile(i, carry):
        tile = start + i
        x0 = tile * SUBLANES
        here = pl.ds(pl.multiple_of(x0, SUBLANES), SUBLANES)
        above = pl.ds(pl.multiple_of(jnp.maximum(x0 - SUBLANES, 0), SUBLANES), SUBLANES)
        below = pl.ds(
            pl.multiple_of(jnp.minimum(x0 + SUBLANES, columns - SUBLANES), SUBLANES), SUBLANES
        )
        top, bottom = tile == 0, tile == end
        to, lane0 = y_place(depth, tile)
        y_rows = pl.ds(pl.multiple_of(to, SUBLANES), SUBLANES)
        y_halos = [y[y_rows, :] for y in y_refs]
        y_lane = jnp.full((SUBLANES, LANES), lane0 + jnp.where(even_y, 1, 0), jnp.int32)
        plane = [
            jnp.where(first_z, 0.0, jnp.where(even_z, z_b[here, at], z_a[here, at])) for at in cuts
        ]
        after = [
            jnp.where(last_z, 0.0, jnp.where(even_z, z_a[here, at], z_b[here, at])) for at in cuts
        ]
        current = [density_ref[0, here, at] for at in cuts]
        sums = [[jnp.zeros((SUBLANES, LANES), jnp.float32) for _ in range(3)] for _ in cuts]
        for z in range(depth):
            following = [density_ref[z + 1, here, at] for at in cuts] if z + 1 < depth else after
            edges = [
                jnp.take_along_axis(y, y_lane + z, axis=1, mode="promise_in_bounds")
                for y in y_halos
            ]
            y_before = y_after = edges[0]
            if len(edges) == 2:
                y_before = jnp.where(even_y, edges[1], edges[0])
                y_after = jnp.where(even_y, edges[0], edges[1])
            y_before, y_after = jnp.where(first_y, 0.0, y_before), jnp.where(last_y, 0.0, y_after)
            right = [pltpu.roll(v, 1, 1) for v in current]
            left = [pltpu.roll(v, LANES - 1, 1) for v in current]
            for p, at in enumerate(cuts):
                low = right[p - 1] if p > 0 else y_before
                high = left[p + 1] if p + 1 < len(cuts) else y_after
                slope_row = jnp.where(lane == LANES - 1, high, left[p]) - jnp.where(
                    lane == 0, low, right[p]
                )
                before = jnp.where(top, x_before[z : z + 1, at], density_ref[z, above, at])
                beyond = jnp.where(bottom, x_after[z : z + 1, at], density_ref[z, below, at])
                slope_column = pltpu.roll(
                    jnp.where(sub == 0, beyond, current[p]), SUBLANES - 1, 0
                ) - pltpu.roll(jnp.where(sub == SUBLANES - 1, before, current[p]), 1, 0)
                slope_depth = following[p] - plane[p]
                facing = 0.48 * slope_depth + 0.36 * slope_column + 0.45 * slope_row
                square = (
                    slope_depth * slope_depth
                    + slope_column * slope_column
                    + (slope_row * slope_row + 4.0)
                )
                shade = 0.25 + jnp.abs(facing) * lax.rsqrt(square)
                for c in range(3):
                    sums[p][c] = sums[p][c] + shade * weighted[c, z, here, at]
            plane, current = current, following
        to = pl.ds(pl.multiple_of(i * SUBLANES, SUBLANES), SUBLANES)
        for p, at in enumerate(cuts):
            for c in range(3):
                out[c, to, at] = sums[p][c]
            out[3, to, at] = depth_in[here, at]
        return carry

    lax.fori_loop(0, tiles, one_tile, 0, unroll=tiles <= 2)


def compose_kernel(count, earlier, *refs):
    out = refs[-1]
    bricks = refs[:count] if len(refs) > 2 else [refs[0].at[i] for i in range(count)]
    depths = [b[3] for b in bricks]
    sums = [jnp.zeros_like(depths[0]) for _ in range(3)]
    total = jnp.zeros_like(depths[0])
    for i, brick in enumerate(bricks):
        prefix = jnp.zeros_like(total)
        for j in range(count):
            if j != i:
                k = i * count + j
                prefix = prefix + earlier[k : k + 1, :] * depths[j]
        left = jnp.exp2(-prefix)
        sums = [s + left * brick[c] for c, s in enumerate(sums)]
        total = total + depths[i]
    for c in range(3):
        out[c] = sums[c]
    out[3] = 1.0 - jnp.exp2(-total)


def swap(values, axis):
    sizes = [lax.axis_size(a) for a in AXES]
    at, other = AXES.index(axis), 0
    strides = [sizes[1] * sizes[2], sizes[2], 1]
    got = []
    for start, value in enumerate(values):
        pairs = []
        for device in range(sizes[0] * sizes[1] * sizes[2]):
            where = [device // s % n for s, n in zip(strides, sizes)]
            partner = where[at] + 1 if where[at] % 2 == start else where[at] - 1
            if 0 <= partner < sizes[at]:
                where[at] = partner
            elif axis == "gx":
                where[at] = sizes[at] - 1 - where[at]
            else:
                where[other] ^= 1
            pairs.append((device, sum(w * s for w, s in zip(where, strides))))
        got.append(lax.ppermute(value, AXES, pairs))
    return got


def local(density, bins, colour_table, opacity_table, order):
    depth, columns, rows = density.shape
    bricks = lax.axis_size("gz")
    near = lambda *shape: pltpu.VMEM(shape, jnp.float32)
    here = lambda *arrays: [pltpu.with_memory_space_constraint(a, pltpu.VMEM) for a in arrays]
    far = lambda *arrays: [pltpu.with_memory_space_constraint(a, pltpu.HBM) for a in arrays]
    call = lambda kernel, name, out_shape, in_specs, **more: pl.pallas_call(
        kernel, name=name, out_shape=out_shape, in_specs=in_specs,
        out_specs=jax.tree.map(lambda _: VMEM, out_shape),
        compiler_params=pltpu.CompilerParams(vmem_limit_bytes=SCOPED), **more,
    )
    y_height, _ = y_shape(depth, columns)
    y_sides = 1 if lax.axis_size("gy") == 2 else 2
    z_faces = call(
        depth_faces_kernel, "depth_faces", [near(columns + SUBLANES, rows), near(columns, rows)], [HBM],
        scratch_shapes=[pltpu.SemaphoreType.DMA((4,))],
        cost_estimate=pl.CostEstimate(flops=2 * 10**9, bytes_accessed=2 * 10**6, transcendentals=0),
    )(*far(density))
    density, bins, order, colour_table, opacity_table = here(
        density, bins, order, colour_table, opacity_table
    )
    side_faces = call(
        side_faces_kernel, "side_faces",
        [near(depth, rows), near(2 * depth, rows)]
        + [near(y_height + SUBLANES, LANES)] * y_sides, [VMEM],
        cost_estimate=pl.CostEstimate(flops=7 * 10**8, bytes_accessed=2 * 10**6, transcendentals=0),

    )(density)
    faces = here(*z_faces, *side_faces)
    halos = swap(faces[:2], "gz") + swap(faces[4:], "gy") + swap(faces[2:4], "gx")

    tile_rows = columns // bricks
    direct = tile_rows % SUBLANES == 0
    shifts = [(k, k % (bricks - 1) + 1) for k in range(1, bricks)] + [(0, 0)] if direct else None
    step = 3.0 / (depth * bricks) * math.log2(math.e) / 1024.0
    weighted, depths, earlier = call(
        functools.partial(weights_kernel, step, shifts), "weights",
        [near(3, depth, columns, rows), near(columns, rows), near(bricks * bricks, rows)],
        [VMEM] * 5,
    )(order, density, bins, colour_table, opacity_table)
    weighted, depths, earlier = here(weighted, depths, earlier)
    shade = lambda part, tile: call(
        functools.partial(shade_kernel, part), "shade",
        near(4, tile, rows), [VMEM] * (3 + len(halos)),
        scratch_shapes=[pltpu.VMEM((depth, rows), jnp.float32)] * 2,
    )(density, weighted, depths, *here(*halos))
    if direct:
        received = []
        for shift in shifts:
            part = shade(shift, tile_rows)
            if shift != (0, 0):
                part = lax.ppermute(part, AXES, shifted(shift))
            received.append(part)
    else:
        whole = shade(None, columns)
        cut = jnp.moveaxis(whole.reshape(4, bricks, tile_rows, rows), 1, 0)
        received = [lax.all_to_all(cut, "gz", 0, 0)]
    return call(
        functools.partial(compose_kernel, bricks), "compose",
        jax.ShapeDtypeStruct((4, tile_rows, rows), jnp.float32), [VMEM] * (1 + len(received)),
    )(earlier, *here(*received))


def solution(mesh):
    return jax.shard_map(
        local,
        mesh=mesh,
        in_specs=(P("gz", "gx", "gy"), P("gz", "gx", "gy"), P(), P(), P("gx", "gy", None)),
        out_specs=P(None, ("gx", "gz"), "gy"),
        check_vma=False,
    )
```
